512 devices in a mesh: dp: 128 (over y, z, core), mp: 4 (over x).
Axes of the slice: x: 4, y: 4, z: 16, core: 2. Of those that a mesh axis runs over, the one named last changes fastest.
Arguments:
- dense_input: bfloat16 [16384, 128], P('dp'), may hold values from -6 to 6
- labels: int32 [16384], P('dp'), may hold values 0 or 1
- table: float32 [32768, 8, 128], P('dp'), may hold values from -4 to 4
- adagrad_state: float32 [32768, 8], P('dp'), may hold values from 1e-05 to 0.001
- new_owner: int32 [32768], P('dp'), may hold values from 0 to 127, as said below
- bag_owner: int32 [49152, 1], P('dp'), may hold values from 0 to 127; in each aligned block of 384 rows (0 to 383, 384 to 767, ...) at most 6 rows name the same one
- bag_slot: int32 [49152], P('dp'), may hold values from 0 to 255
- bag_offsets: int32 [49152, 16], P('dp'), may hold values from 0 to 7
- bag_length: int32 [49152], P('dp'), may hold values from 1 to 16
- w_first: bfloat16 [512, 4096], P(None, 'mp'), may hold values from -0.25 to 0.25
- b_first: float32 [4096], P('mp'), may hold values from -3 to 3
- w_out: float32 [4096], P('mp'), may hold values from -0.09375 to 0.09375
Outputs:
- updated_table: float32 [32768, 8, 128], P('dp')
- updated_state: float32 [32768, 8], P('dp')
- grad_w1: bfloat16 [512, 4096], P(None, 'mp')
- grad_b1: float32 [4096], P('mp')
- grad_w2: float32 [4096], P('mp')
The draws below stay inside these ranges and needn't reach their ends.
Inputs may be any that keep to these rules, and one draw needn't show every extreme that they name: `new_owner`: every owner receives exactly 256 blocks; a device sends at most 2 blocks to one owner, and exactly 2 to some owner. `bag_owner`: among the bags of one device, at most 6 name one owner.
All inputs are finite; a program needn't handle non-finite values. No bound on the sum of `labels` on one device may be relied on, other than what follows from the above.
Results may differ from the reference program's by a relative error of at most 0.0052.
Values may be sent and summed in bfloat16 or wider, within the bound.
A program may use at most 64 MiB of HBM per device.

```python
import math
import jax
import jax.numpy as jnp
import numpy as np
from jax import lax

E = 128
H = 4096
NF = 3
RB = 8
L = 16
B_DEV = 128
BLK_DEV = 256
IN = 512
CAP = 2
CAPB = 6
BLOCKS = 32768
SAMPLES = 16384
BAGS = 49152
N_DP = 128


def draw_new_owner(key, part):
    key = jax.random.fold_in(key, 11)
    order_key, slot_key = jax.random.split(key, 2)
    offset_ids = jnp.arange(N_DP, dtype=jnp.int32)
    shuffled = jax.random.permutation(order_key, N_DP).astype(jnp.int32)
    scores = shuffled + 2 * N_DP * (offset_ids != 1).astype(jnp.int32) + N_DP * (offset_ids != N_DP // 2).astype(jnp.int32)
    ranked = jnp.argsort(scores, stable=True).astype(jnp.int32)
    offsets = jnp.repeat(ranked, CAP)[:BLK_DEV]
    slot_perms = jax.vmap(lambda one_key: jax.random.permutation(one_key, BLK_DEV))(jax.random.split(slot_key, N_DP))
    device_ids = jnp.arange(N_DP, dtype=jnp.int32)[:, None]
    owners = (device_ids + offsets[slot_perms]) % N_DP
    return owners.reshape(-1).astype(jnp.int32)


def plant(array, own_key, smallest, largest):
    longest = array.shape.index(max(array.shape))
    spots = []
    for shift in (0, 1):
        where = [jax.random.randint(jax.random.fold_in(own_key, axis), (), 0, length) for axis, length in enumerate(array.shape)]
        where[longest] = (where[longest] + shift) % array.shape[longest]
        spots.append(tuple(where))
    return array.at[spots[0]].set(smallest).at[spots[1]].set(largest)


def steps_of(rng, shape, pieces, least, high):
    def one(axis_at, shards_of):
        steps = jax.random.uniform(jax.random.fold_in(jax.random.fold_in(rng, 6), axis_at), (shards_of,), jnp.float32, least / len(pieces), high / len(pieces))
        return jnp.repeat(jnp.exp(steps), shape[axis_at] // shards_of).reshape((-1,) + (1,) * (len(shape) - axis_at - 1))

    level = one(*pieces[0])
    for cut in pieces[1:]:
        level = level * one(*cut)
    return level


def shared_out(stream_key, own, number, rows, number_of, top, most, skew):
    ranking = jax.random.permutation(stream_key, number_of)
    packed, ordinary = load_shares(number_of, rows * top, most, skew, True), load_shares(number_of, rows * top, most, skew, False)
    places = jnp.arange(number_of)

    def named(tallies, turn):
        used = int((tallies > 0).sum())
        fixed = max(1, used // 4)
        passed = fixed + (places - fixed + turn * (used - fixed)) % max(1, number_of - fixed)
        return jnp.zeros((number_of,), jnp.int32).at[ranking[jnp.where(places < fixed, places, passed)]].set(jnp.asarray(tallies, jnp.int32))

    tallies = jnp.where(number % 4 == 0, named(packed, number // 4), named(ordinary, number - number // 4 - 1))
    mixed = jax.random.permutation(jax.random.fold_in(own, 3), number_of)
    source_of, taker = mixed[0:number_of // 2 * 2:2], mixed[1:number_of // 2 * 2:2]
    margin = jnp.minimum(tallies[source_of] - 1, most - tallies[taker]) // 2
    margin = jnp.where((source_of == ranking[0]) | (taker == ranking[0]) | (tallies[taker] == 0), 0, jnp.maximum(margin, 0))
    passed = jax.random.randint(jax.random.fold_in(own, 4), (number_of // 2,), 0, 1 << 20) % (margin + 1)
    tallies = tallies.at[source_of].add(-passed).at[taker].add(passed)
    items = jnp.searchsorted(jnp.cumsum(tallies), jnp.arange(rows * top), side="right").astype(jnp.int32)
    listing = items.reshape(top, rows).T
    listing = listing[jax.random.permutation(jax.random.fold_in(own, 1), rows)]
    turn = jax.random.randint(jax.random.fold_in(own, 2), (rows, 1), 0, top)
    return jnp.take_along_axis(listing, (jnp.arange(top)[None, :] + turn) % top, axis=1)


def load_shares(amount, total, bound, lean, full):
    weights = [(1 << 20) // math.isqrt(standing ** lean) + 1 for standing in range(1, amount + 1)]
    largest = bound if full else min(bound, max(-(-total // amount), total * weights[0] // sum(weights)))
    least = 1 if total - largest >= amount - 1 else 0
    given, spare = [largest] + [least] * (amount - 1), total - largest - least * (amount - 1)
    while spare > 0:
        candidates = [i for i in range(1, amount) if given[i] < largest] or [i for i in range(1, amount) if given[i] < bound]
        pool, budget = sum([weights[i] for i in candidates]), spare
        for i in candidates:
            extra = min(bound - given[i], max(1, budget * weights[i] // pool), spare)
            given[i] = given[i] + extra
            spare = spare - extra
    return np.array(given)


def scatter_about(rng, dims, scale, most, cuts=(), kind=jnp.bfloat16):
    array = scale * jax.random.normal(rng, dims, jnp.float32)
    if cuts:
        array = array * steps_of(rng, dims, cuts, -0.22, 0.18)
    return jnp.clip(array, -most, most).astype(kind)


def setup_inputs(seed: int = 0) -> dict:
    streams_of = jax.random.split(jax.random.key(seed), 13)
    dense_input = scatter_about(streams_of[0], (SAMPLES, E), 1.0, 6.0, ((0, 128),))
    labels = plant((jax.random.randint(streams_of[1], (SAMPLES,), 0, 2) < 1).astype(jnp.int32), jax.random.fold_in(streams_of[1], 1), 0, 1)
    table = scatter_about(streams_of[2], (BLOCKS, RB, E), 0.5, 4.0, ((0, 128),), jnp.float32)
    adagrad_state = jnp.clip(jnp.exp(math.log(0.001) - 4.6051703 * jax.random.uniform(streams_of[3], (BLOCKS, RB), jnp.float32) ** steps_of(streams_of[3], (BLOCKS, RB), ((0, 128),), -0.2, 0.2)), 9.999999747378752e-06, 0.001)
    new_owner = draw_new_owner(jax.random.fold_in(streams_of[12], 71), 0)
    bag_owner_keys = jax.random.split(jax.random.fold_in(streams_of[5], 1), BAGS // (B_DEV * NF))
    bag_owner_turns = jax.random.permutation(jax.random.fold_in(streams_of[5], 3), BAGS // (B_DEV * NF))
    bag_owner = jax.vmap(lambda own, number: shared_out(jax.random.fold_in(streams_of[5], 2), own, number, B_DEV * NF, N_DP, 1, CAPB, 2))(bag_owner_keys, bag_owner_turns).reshape((BAGS, 1))
    bag_slot = plant(jax.random.randint(streams_of[6], (BAGS,), 0, BLK_DEV), jax.random.fold_in(streams_of[6], 1), 0, BLK_DEV - 1).astype(jnp.int32)
    bag_offsets = plant(jax.random.randint(streams_of[7], (BAGS, L), 0, RB), jax.random.fold_in(streams_of[7], 1), 0, RB - 1).astype(jnp.int32)
    bag_length = plant(jax.random.randint(streams_of[8], (BAGS,), 1, L + 1), jax.random.fold_in(streams_of[8], 1), 1, L).astype(jnp.int32)
    w_first = scatter_about(streams_of[9], (IN, H), IN ** -0.5, 0.25, ((1, 4),))
    b_first = scatter_about(streams_of[10], (H,), 0.5, 3.0, ((0, 4),), jnp.float32)
    w_out = scatter_about(streams_of[11], (H,), H ** -0.5, 0.09375, ((0, 4),), jnp.float32)
    return dict(dense_input=dense_input, labels=labels, table=table, adagrad_state=adagrad_state, new_owner=new_owner, bag_owner=bag_owner, bag_slot=bag_slot, bag_offsets=bag_offsets, bag_length=bag_length, w_first=w_first, b_first=b_first, w_out=w_out)


learn_rate = 0.01
epsilon = 1e-08

def silu_slope(pre_act):
    sigmoid_val = jax.nn.sigmoid(pre_act)
    return sigmoid_val * (1.0 + pre_act * (1.0 - sigmoid_val))

def reference(dense_input, labels, table, adagrad_state, new_owner, bag_owner, bag_slot, bag_offsets, bag_length, w_first, b_first, w_out):
    order_index = jnp.argsort(new_owner, stable=True)
    moved_rows = table[order_index]
    moved_state = adagrad_state[order_index]
    low_table = moved_rows.reshape(BLOCKS * RB, E).astype(jnp.bfloat16)
    lane_ids = jnp.arange(L, dtype=jnp.int32)[None, :]
    row_index = ((bag_owner[:, 0] * BLK_DEV + bag_slot)[:, None] * RB + bag_offsets).astype(jnp.int32)
    live_mask = lane_ids < bag_length[:, None]
    group_index = row_index.reshape(N_DP, B_DEV * NF, L)
    group_mask = live_mask.reshape(N_DP, B_DEV * NF, L)
    dense_groups = dense_input.reshape(N_DP, B_DEV, E)
    label_groups = labels.reshape(N_DP, B_DEV).astype(jnp.float32)
    tail_weight = w_first[E:]

    def one_group(carry, inputs):
        grad_rows, sum_w1, sum_w2, sum_b1 = carry
        index_rows, mask_rows, dense_rows, label_rows = inputs
        gathered = low_table[index_rows].astype(jnp.float32)
        pooled = lax.optimization_barrier(jnp.sum(jnp.where(mask_rows[:, :, None], gathered, 0.0), axis=1)).astype(jnp.bfloat16)
        features = jnp.concatenate([dense_rows, pooled.reshape(B_DEV, NF * E)], axis=1)
        hidden_pre = jnp.dot(features, w_first, preferred_element_type=jnp.float32) + b_first
        active = jax.nn.silu(hidden_pre)
        logit_vals = jnp.dot(active, w_out, precision=lax.Precision.HIGHEST)
        logit_grad = jax.nn.sigmoid(logit_vals) - label_rows
        grad_pre = logit_grad[:, None] * w_out[None, :] * silu_slope(hidden_pre)
        grad_low = grad_pre.astype(jnp.bfloat16)
        sum_w1 = sum_w1 + jnp.dot(features.T, grad_low, preferred_element_type=jnp.float32)
        sum_w2 = sum_w2 + jnp.dot(logit_grad, active, precision=lax.Precision.HIGHEST)
        sum_b1 = sum_b1 + lax.optimization_barrier(jnp.sum(grad_pre, axis=0))
        part_input = jnp.dot(grad_low, tail_weight.T, preferred_element_type=jnp.float32)
        bag_grad = part_input.reshape(B_DEV * NF, E)
        spread = jnp.where(mask_rows[:, :, None], bag_grad[:, None, :], 0.0)
        grad_rows = grad_rows.at[index_rows.reshape(-1)].add(spread.reshape(-1, E))
        return ((grad_rows, sum_w1, sum_w2, sum_b1), None)
    start_sum = (jnp.zeros((BLOCKS * RB, E), jnp.float32), jnp.zeros((IN, H), jnp.float32), jnp.zeros((H,), jnp.float32), jnp.zeros((H,), jnp.float32))
    totals, unused = lax.scan(one_group, start_sum, (group_index, group_mask, dense_groups, label_groups))
    grad_rows, sum_w1, sum_w2, sum_b1 = totals
    grad_rows = grad_rows.reshape(BLOCKS, RB, E)
    updated_state = moved_state + lax.optimization_barrier(jnp.mean(grad_rows * grad_rows, axis=2))
    updated_table = moved_rows - learn_rate * grad_rows / (jnp.sqrt(updated_state)[:, :, None] + epsilon)
    return (updated_table, updated_state, sum_w1.astype(jnp.bfloat16), sum_b1, sum_w2)
```

```python
import functools

import jax
import jax.numpy as jnp
from jax import lax
from jax.experimental import pallas as pl
from jax.experimental.pallas import tpu as pltpu
from jax.sharding import PartitionSpec as P

MESH = pl.DeviceIdType.MESH
BF = jnp.bfloat16
F32 = jnp.float32
I32 = jnp.int32
learn_rate = 0.01
epsilon = 1e-08
W = 128


def iota(shape, dim):
    return lax.broadcasted_iota(I32, shape, dim)


def dot(a, b, dims=((1,), (0,)), exact=False):
    return lax.dot_general(
        a,
        b,
        (dims, ((), ())),
        precision=lax.Precision.HIGHEST if exact else None,
        preferred_element_type=F32,
    )


def log2(n):
    return n.bit_length() - 1


def onehot(mask):
    return jnp.where(mask, 1.0, 0.0).astype(BF)


def to_col(row, rows, pick):
    return jnp.sum(jnp.where(pick, row, 0.0), axis=1, keepdims=True)


class Shape:
    def __init__(self, dp, mp, blocks, samples, hidden):
        self.C = 2
        self.Y = 4 if dp == 128 else 2
        self.Z = dp // (self.C * self.Y)
        self.M = mp
        self.K = self.Z // mp
        self.G = self.Y * self.C
        self.N = dp
        self.NB = blocks
        self.B = samples
        self.HL = hidden
        self.T = self.G * self.K
        self.RY = 512 // (self.C * self.Y)
        self.RG = min(self.Z, self.RY // 16)
        self.CG = self.Z // self.RG
        self.pr = self.RY // self.RG
        self.pc = hidden // self.CG
        self.V = hidden // (W * self.Y)


def kernel(
    S,
    owner_ref,
    bown_ref,
    bslot_ref,
    boff_ref,
    blen_ref,
    dense_ref,
    label_ref,
    table_ref,
    state_ref,
    w_ref,
    b_ref,
    wo_ref,
    out_t,
    out_s,
    out_w,
    out_v,
    stage_t,
    send_t,
    send_r,
    mid_t,
    mid_r,
    recv_t,
    recv_r,
    rmat,
    pooled,
    mid_p,
    send_p,
    slots,
    lbuf,
    act,
    slope,
    feat,
    part_s,
    recv_x,
    send_g,
    mid_g,
    send_h,
    recv_g,
    send_c,
    keep_c,
    recv_c,
    send_y,
    keep_y,
    recv_y,
    send_z,
    recv_z,
    vec,
    vec_c,
    vec_y,
    vec_ys,
    vec_z,
    ss,
    rs,
    sr,
    rr,
):
    C, Y, Z, M, K, G, N, NB, B, HL, T = S.C, S.Y, S.Z, S.M, S.K, S.G, S.N, S.NB, S.B, S.HL, S.T
    B3 = 3 * B
    NS = N * 8
    lY, lZ, lM, lK, lG = log2(Y), log2(Z), log2(M), log2(K), log2(G)
    me = lax.axis_index("dp")
    m = lax.axis_index("mp")
    c = lax.rem(me, C)
    z = lax.rem(me // C, Z)
    y = me // (C * Z)
    g = y * C + c
    half = M // 2
    home = lax.rem(z + half * c, M)
    conc = home == m
    base_z = lax.rem(m + M - half * c, M)

    def dp_of(gg, zz):
        return ((gg // C) * Z + zz) * C + lax.rem(gg, C)

    def remote(src, dst, i, dp, mp, small=False):
        pltpu.make_async_remote_copy(
            src_ref=src,
            dst_ref=dst,
            send_sem=(sr if small else ss).at[i],
            recv_sem=(rr if small else rs).at[i],
            device_id=(dp, mp),
            device_id_type=MESH,
        ).start()

    def local(src, dst, i, small=False):
        pltpu.make_async_copy(src, dst, (rr if small else rs).at[i]).start()

    def wait_in(ref, i, small=False):
        pltpu.make_async_copy(ref, ref, (rr if small else rs).at[i]).wait()

    def wait_out(ref, i, small=False):
        pltpu.make_async_copy(ref, ref, (sr if small else ss).at[i]).wait()

    def each(lo, hi, body):
        def step(t, carry):
            body(t)
            return carry

        lax.fori_loop(lo, hi, step, 0)

    barrier = pltpu.get_barrier_semaphore()

    def greet(dp, mp):
        pl.semaphore_signal(barrier, inc=1, device_id=(dp, mp), device_id_type=MESH)

    each(1, G, lambda t: greet(dp_of(lax.rem(g + t, G), z), m))
    each(1, Z, lambda t: greet(dp_of(g, lax.rem(z + t, Z)), m))
    each(1, M, lambda t: greet(me, lax.rem(m + t, M)))

    def target_of(tt):
        gg = lax.shift_right_logical(tt, lK)
        kk = tt & (K - 1)
        yy = lax.shift_right_logical(gg, 1)
        cc = gg & 1
        zz = ((m + M - half * cc) & (M - 1)) + M * kk
        return (yy * Z + zz) * C + cc

    own_row = owner_ref[...].astype(F32)
    own_col = to_col(own_row, NB, iota((NB, NB), 0) == iota((NB, NB), 1))
    rank_row = jnp.sum(
        jnp.where((own_col == own_row) & (iota((NB, NB), 0) < iota((NB, NB), 1)), 1.0, 0.0),
        axis=0,
        keepdims=True,
    )
    rows2 = iota((2 * T, 1), 0)
    want = target_of(lax.shift_right_logical(rows2, 1)).astype(F32)
    pick_f = jnp.where((own_row == want) & (rank_row == (rows2 & 1).astype(F32)), 1.0, 0.0)
    pick = pick_f.astype(BF)
    for r in range(8):
        low = table_ref[pl.ds(r, NB, stride=8), :].astype(BF)
        stage_t[pl.ds(r, 2 * T, stride=8), :] = dot(pick, low)
    send_t[...] = stage_t[...].astype(BF).reshape(G, K, 16, W)

    bo_row = bown_ref[...].astype(F32)
    eye = iota((B3, B3), 0) == iota((B3, B3), 1)
    bo_col = to_col(bo_row, B3, eye)
    same = bo_col == bo_row
    brank_col = jnp.sum(jnp.where(same & (iota((B3, B3), 1) < iota((B3, B3), 0)), 1.0, 0.0), axis=1, keepdims=True)
    brank_row = jnp.sum(jnp.where(same & (iota((B3, B3), 0) < iota((B3, B3), 1)), 1.0, 0.0), axis=0, keepdims=True)
    slot_nat = bslot_ref[...]
    sy = lax.shift_right_logical(slot_nat, lZ + 2)
    sz = lax.shift_right_logical(slot_nat, 2) & (Z - 1)
    slot_z = ((sz * Y + sy) * 4 + (slot_nat & 3)).astype(F32)
    slot_col = to_col(slot_z, B3, eye)
    len_col = to_col(blen_ref[...].astype(F32), B3, eye)
    lane = iota((B3, W), 1)
    spread = onehot((iota((16, W), 1) & 15) == iota((16, W), 0))
    off_t = dot(boff_ref[...].astype(F32).astype(BF), spread)
    hit = onehot((off_t == lax.shift_right_logical(lane, 4).astype(F32)) & ((lane & 15).astype(F32) < len_col))
    gather8 = onehot((iota((W, W), 1) & 15) == lax.shift_right_logical(iota((W, W), 0), 4))
    counts = dot(hit, gather8)
    req = jnp.where((lane & 15) == 8, slot_col, counts)
    req = jnp.where(lax.shift_right_logical(lane, 4).astype(F32) == brank_col, req, 0.0).astype(BF)
    want_t = target_of(iota((T, 1), 0)).astype(F32)
    rows = dot(onehot(bo_row == want_t), req)
    for p in range(2):
        put = jnp.where(iota((8, W), 1) == iota((8, W), 0) + 96 + 8 * p, 1.0, 0.0)
        placed = dot(state_ref[...], put, exact=True)
        pick_p = jnp.where((own_row == want_t) & (rank_row == float(p)), 1.0, 0.0)
        rows = rows + dot(pick_p, placed, exact=True)
    for t in range(T):
        send_r[t // K, t % K] = rows[t : t + 1, :]

    pl.semaphore_wait(barrier, (G - 1) + (Z - 1) + (M - 1))

    local(send_r.at[g], mid_r.at[g], 0, True)
    local(send_t.at[g], mid_t.at[g], 0)

    def fwd_a(t):
        gg = lax.rem(g + t, G)
        remote(send_r.at[gg], mid_r.at[g], 0, dp_of(gg, z), m, True)
        remote(send_t.at[gg], mid_t.at[g], 0, dp_of(gg, z), m)

    each(1, G, fwd_a)
    wait_in(mid_r, 0, True)
    wait_in(mid_t, 0)

    def fwd_b(k):
        zz = base_z + M * k

        @pl.when(zz != z)
        def _():
            remote(mid_r.at[:, k], recv_r.at[z], 1, dp_of(g, zz), m, True)
            remote(mid_t.at[:, k], recv_t.at[z], 1, dp_of(g, zz), m)

        @pl.when(zz == z)
        def _():
            local(mid_r.at[:, k], recv_r.at[z], 1, True)
            local(mid_t.at[:, k], recv_t.at[z], 1)

    each(0, K, fwd_b)

    bo = bown_ref[...]
    oc = bo & 1
    oz = lax.shift_right_logical(bo, 1) & (Z - 1)
    oy = lax.shift_right_logical(bo, 1 + lZ)
    om = (oz + half * oc) & (M - 1)
    ok = lax.shift_right_logical(oz, lM)
    place = (((om * G + oy * C + oc) * K + ok) * 8).astype(F32) + brank_row
    pcol, prow = [], []
    for f in range(3):
        col = to_col(place, B, iota((B, B3), 1) == 3 * iota((B, B3), 0) + f)
        pcol.append(col)
        prow.append(jnp.sum(jnp.where(iota((B, B), 0) == iota((B, B), 1), col, 0.0), axis=0, keepdims=True))

    pick16 = lax.shift_right_logical(iota((W, W), 0), 4)
    low16 = iota((W, W), 0) & 15
    tile_c = onehot(low16 == (iota((W, W), 1) & 7))
    tile_s = onehot(low16 == 8)
    del pick16

    def flat_rows():
        def one(i):
            rmat[pl.ds(i, 1), :] = recv_r[i // G, lax.rem(i, G)]

        each(0, N, one)

    CH = min(NS, 2 * G * 8)

    def entries(i, n):
        row = iota((n, N), 0) + i * n
        src = onehot(lax.shift_right_logical(row, 3) == iota((n, N), 1))
        wide = dot(src, jnp.where(iota((N, W), 1) < 96, rmat[...], 0.0).astype(BF))
        keep = lax.shift_right_logical(iota((n, W), 1), 4) == (iota((n, W), 0) & 7)
        return jnp.where(keep, wide, 0.0).astype(BF)

    @pl.when(conc)
    def _():
        wait_in(recv_r, 1, True)
        wait_in(recv_t, 1)

        def cast(t):
            remote(recv_r, recv_r, 2, me, lax.rem(m + t, M), True)
            remote(recv_t, recv_t, 2, me, lax.rem(m + t, M))

        each(1, M, cast)
        flat_rows()

        def pool(i):
            ent = entries(i, CH)
            cnt = dot(ent, tile_c)
            slt = dot(ent, tile_s)
            group = lax.shift_right_logical(iota((CH, W), 1), 3)
            parts = [
                jnp.where(slt == (group + 16 * q).astype(F32), cnt, 0.0).astype(BF) for q in range(NB // 16)
            ]
            wide = jnp.concatenate(parts, axis=1) if len(parts) > 1 else parts[0]
            got = dot(wide, recv_t[...].reshape(NB * 8, W))
            per = CH // (G * 8)
            pooled[pl.ds(i * per, per)] = got.astype(BF).reshape(per, G * 8, W)

            def send(q):
                zz = i * per + q

                @pl.when(zz != z)
                def _():
                    remote(pooled.at[zz], mid_p.at[z // M], 3, dp_of(g, zz), m)

                @pl.when(zz == z)
                def _():
                    local(pooled.at[zz], mid_p.at[z // M], 3)

            each(0, per, send)

        each(0, NS // CH, pool)

    wait_in(mid_p, 3)
    R2 = K * G * 8
    ro = iota((R2, R2), 0)
    ri = iota((R2, R2), 1)
    swap = (
        (lax.shift_right_logical(ro, lK + 3) == (lax.shift_right_logical(ri, 3) & (G - 1)))
        & ((lax.shift_right_logical(ro, 3) & (K - 1)) == lax.shift_right_logical(ri, lG + 3))
        & ((ro & 7) == (ri & 7))
    )
    send_p[...] = dot(onehot(swap), mid_p[...].reshape(R2, W)).astype(BF).reshape(G, K * 8, W)
    local(send_p.at[g], slots.at[m, g], 4)

    def ret_a(t):
        gg = lax.rem(g + t, G)
        remote(send_p.at[gg], slots.at[m, g], 4, dp_of(gg, z), m)

    each(1, G, ret_a)
    wait_in(slots.at[m], 4)
    each(1, M, lambda t: remote(slots.at[m], slots.at[m], 5, me, lax.rem(m + t, M)))
    wait_in(slots.at[pl.ds(0, M - 1)], 5)

    table_s = slots[...].reshape(NS, W)
    feat[0] = dense_ref[...]
    for f in range(3):
        feat[f + 1] = dot(onehot(iota((B, NS), 1).astype(F32) == pcol[f]), table_s).astype(BF)
    features = jnp.concatenate([feat[i] for i in range(4)], axis=1)
    pre = dot(features, w_ref[...]) + b_ref[...]
    sig = jax.nn.sigmoid(pre)
    active = pre * sig
    act[...] = active
    slope[...] = sig * (1.0 + pre * (1.0 - sig)) * wo_ref[...]
    part = jnp.sum(active * wo_ref[...], axis=1, keepdims=True)
    eye_b = iota((B, B), 0) == iota((B, B), 1)
    part_row = jnp.sum(jnp.where(eye_b, part, 0.0), axis=0, keepdims=True)
    lbuf[m] = jnp.broadcast_to(part_row, (8, B))
    each(1, M, lambda t: remote(lbuf.at[m], lbuf.at[m], 3, me, lax.rem(m + t, M), True))
    wait_in(lbuf.at[pl.ds(0, M - 1)], 3, True)

    total = lbuf[0]
    for i in range(1, M):
        total = total + lbuf[i]
    lgrad_row = jax.nn.sigmoid(total[0:1, :]) - label_ref[...].astype(F32)
    lgrad = to_col(lgrad_row, B, eye_b)
    grad_pre = lgrad * slope[...]
    grad_low = grad_pre.astype(BF)
    b1 = jnp.sum(grad_pre, axis=0, keepdims=True)
    w2 = jnp.sum(lgrad * act[...], axis=0, keepdims=True)
    for i, row in enumerate((b1, w2)):
        for j in range(HL // W):
            vec[i, j // S.V, pl.ds(j % S.V, 1), :] = row[:, j * W : (j + 1) * W]

    hrows = 512 // C
    other = 1 - c
    mate = me + 1 - 2 * c

    def term_of(i, blk):
        return dot(feat[i], blk, ((0,), (0,)))

    for h in range(C):

        @pl.when(c != h)
        def _():
            for i in range(2):
                send_c[pl.ds(i * W, W), :] = term_of(2 * h + i, grad_low).astype(BF)

        @pl.when(c == h)
        def _():
            for i in range(2):
                keep_c[pl.ds(i * W, W), :] = term_of(2 * h + i, grad_low)

    remote(send_c, recv_c, 6, mate, m)
    remote(vec.at[other], vec_c, 6, mate, m, True)

    inputs = [
        dot(grad_low, w_ref[pl.ds((f + 1) * W, W), :], ((1,), (1,))).astype(BF) for f in range(3)
    ]
    for q in range(M):
        acc = None
        for f in range(3):
            rowid = (iota((R2, B), 0) + q * R2).astype(F32)
            term = dot(onehot(rowid == prow[f]), inputs[f])
            acc = term if acc is None else acc + term
        part_s[q] = acc.astype(BF)

    def xrs(t):
        mm = lax.rem(m + t, M)
        remote(part_s.at[mm], recv_x.at[m], 7, me, mm)

    local(part_s.at[m], recv_x.at[m], 7)
    each(1, M, xrs)

    wait_in(recv_c, 6)
    wait_in(vec_c, 6, True)
    keep_y[...] = keep_c[...] + recv_c[...].astype(F32)
    send_y[...] = keep_y[...].astype(BF).reshape(Y, S.RY, HL)
    vec[c] = vec[c] + vec_c[...]

    def to_y(t):
        yy = lax.rem(y + t, Y)
        remote(send_y.at[yy], recv_y.at[y], 8, (yy * Z + z) * C + c, m)
        remote(vec.at[c, yy], vec_y.at[y], 8, (yy * Z + z) * C + c, m, True)

    each(1, Y, to_y)

    wait_in(recv_x, 7)
    acc = recv_x[0].astype(F32)
    for i in range(1, M):
        acc = acc + recv_x[i].astype(F32)
    send_g[...] = acc.astype(BF).reshape(G, K * 8, W)
    local(send_g.at[g], mid_g.at[g], 9)

    def grad_a(t):
        gg = lax.rem(g + t, G)
        remote(send_g.at[gg], mid_g.at[g], 9, dp_of(gg, z), m)

    each(1, G, grad_a)

    wait_in(recv_y.at[pl.ds(0, Y - 1)], 8)
    wait_in(vec_y.at[pl.ds(0, Y - 1)], 8, True)
    acc = keep_y[pl.ds(pl.multiple_of(y * S.RY, S.RY), S.RY), :]
    accv = vec[c, y]
    for t in range(1, Y):
        yy = lax.rem(y + t, Y)
        acc = acc + recv_y[yy].astype(F32)
        accv = accv + vec_y[yy]
    for i in range(Z):
        r0, c0 = (i // S.CG) * S.pr, (i % S.CG) * S.pc
        send_z[i] = acc[r0 : r0 + S.pr, c0 : c0 + S.pc].astype(BF)
    vec_ys[...] = accv
    local(send_z.at[z], recv_z.at[z], 10)
    local(vec_ys, vec_z.at[z], 10, True)

    def to_z(t):
        zz = lax.rem(z + t, Z)
        remote(send_z.at[zz], recv_z.at[z], 10, dp_of(g, zz), m)
        remote(vec_ys, vec_z.at[z], 10, dp_of(g, zz), m, True)

    each(1, Z, to_z)

    wait_in(mid_g, 9)
    unswap = (
        (lax.shift_right_logical(ri, lK + 3) == (lax.shift_right_logical(ro, 3) & (G - 1)))
        & ((lax.shift_right_logical(ri, 3) & (K - 1)) == lax.shift_right_logical(ro, lG + 3))
        & ((ro & 7) == (ri & 7))
    )
    send_h[...] = dot(onehot(unswap), mid_g[...].reshape(R2, W)).astype(BF).reshape(K, G * 8, W)

    def grad_b(k):
        zz = base_z + M * k

        @pl.when(zz != z)
        def _():
            remote(send_h.at[k], recv_g.at[z], 11, dp_of(g, zz), m)

        @pl.when(zz == z)
        def _():
            local(send_h.at[k], recv_g.at[z], 11)

    each(0, K, grad_b)

    wait_in(recv_z, 10)
    wait_in(vec_z, 10, True)

    def add_z(i, carry):
        return carry[0] + recv_z[i].astype(F32), carry[1] + vec_z[i]

    acc, accv = lax.fori_loop(
        0, Z, add_z, (jnp.zeros((S.pr, S.pc), F32), jnp.zeros((S.V, W), F32))
    )
    block0 = c * hrows + y * S.RY

    def piece(yy, zz):
        r0 = pl.multiple_of(c * hrows + yy * S.RY + (zz // S.CG) * S.pr, 16)
        c0 = pl.multiple_of(lax.rem(zz, S.CG) * S.pc, W)
        return out_w.at[pl.ds(r0, S.pr), pl.ds(c0, S.pc)]

    out_w[
        pl.ds(pl.multiple_of(block0 + (z // S.CG) * S.pr, 16), S.pr),
        pl.ds(pl.multiple_of(lax.rem(z, S.CG) * S.pc, W), S.pc),
    ] = acc.astype(BF)
    out_v[c, y] = accv
    each(1, Z, lambda t: remote(piece(y, z), piece(y, z), 12, dp_of(g, lax.rem(z + t, Z)), m))

    @pl.when(conc)
    def _():
        wait_in(recv_g, 11)
        each(1, M, lambda t: remote(recv_g, recv_g, 13, me, lax.rem(m + t, M)))

    wait_in(send_z.at[pl.ds(0, Z - 1)], 12)
    mine = out_w.at[pl.ds(pl.multiple_of(block0, 16), S.RY), :]

    def ag_y(t):
        yy = lax.rem(y + t, Y)
        remote(mine, mine, 14, (yy * Z + z) * C + c, m)
        remote(out_v.at[c, y], out_v.at[c, y], 14, (yy * Z + z) * C + c, m, True)

    each(1, Y, ag_y)

    @pl.when(jnp.logical_not(conc))
    def _():
        wait_in(recv_r, 2, True)
        wait_in(recv_t, 2)
        flat_rows()
        wait_in(recv_g, 13)

    wait_in(send_y.at[pl.ds(0, Y - 1)], 14)
    wait_in(out_v.at[0, pl.ds(0, Y - 1)], 14, True)
    myhalf = out_w.at[pl.ds(pl.multiple_of(c * hrows, 16), hrows), :]
    remote(myhalf, myhalf, 15, mate, m)
    remote(out_v.at[c], out_v.at[c], 15, mate, m, True)

    sel = onehot((iota((16, W), 1) & 15) == iota((16, W), 0))
    lists = dot(sel, entries(0, NS), ((1,), (1,)))
    cnt8 = lists[0:8, :]
    slot_row = lists[8:9, :]
    grads = recv_g[...].reshape(NS, W)
    QR = G * 16

    def update(i):
        row = iota((QR, 1), 0)
        slot_id = (lax.shift_right_logical(row, 3) + i * (QR // 8)).astype(F32)
        cnt = jnp.broadcast_to(cnt8[None], (QR // 8, 8, NS)).reshape(QR, NS)
        wide = jnp.where(slot_row == slot_id, cnt, 0.0).astype(BF)
        grad = dot(wide, grads)
        src_rows = rmat[pl.ds(pl.multiple_of(i * G, G), G), :]
        wide_s = jnp.broadcast_to(src_rows[:, None, :], (G, 16, W)).reshape(QR, W)
        pick_s = iota((QR, W), 1) == (iota((QR, W), 0) & 15) + 96
        st = jnp.sum(jnp.where(pick_s, wide_s, 0.0), axis=1, keepdims=True)
        st = st + jnp.sum(grad * grad, axis=1, keepdims=True) * (1.0 / W)
        old = recv_t[i].reshape(QR, W).astype(F32)
        new = old - learn_rate * grad / (jnp.sqrt(st) + epsilon)
        pick_o = iota((QR, W), 1) == (iota((QR, W), 0) & 7)
        st8 = jnp.sum(jnp.where(pick_o, st, 0.0).reshape(QR // 8, 8, W), axis=1)
        for q in range(Y):
            out_t[pl.ds(pl.multiple_of((q * Z + i) * 32, 32), 32), :] = new[q * 32 : (q + 1) * 32]
            out_s[q, i] = st8[q * 4 : (q + 1) * 4]

    each(0, Z, update)

    wait_in(recv_c, 15)
    wait_in(vec_c, 15, True)

    wait_out(mid_r.at[pl.ds(0, G - 1)], 0, True)
    wait_out(mid_t.at[pl.ds(0, G - 1)], 0)
    wait_out(mid_g.at[pl.ds(0, G - 1)], 9)
    wait_out(send_p.at[pl.ds(0, G - 1)], 4)
    wait_out(slots.at[pl.ds(0, M - 1)], 5)
    wait_out(lbuf.at[pl.ds(0, M - 1)], 3, True)
    wait_out(send_c, 6)
    wait_out(vec_c, 6, True)
    wait_out(part_s.at[pl.ds(0, M - 1)], 7)
    wait_out(send_y.at[pl.ds(0, Y - 1)], 8)
    wait_out(vec_y.at[pl.ds(0, Y - 1)], 8, True)
    wait_out(send_z.at[pl.ds(0, Z - 1)], 10)
    wait_out(vec_z.at[pl.ds(0, Z - 1)], 10, True)
    wait_out(send_z.at[pl.ds(0, Z - 1)], 12)
    wait_out(send_y.at[pl.ds(0, Y - 1)], 14)
    wait_out(out_v.at[0, pl.ds(0, Y - 1)], 14, True)
    wait_out(recv_c, 15)
    wait_out(vec_c, 15, True)

    @pl.when(conc)
    def _():
        if K > 1:
            wait_out(recv_r.at[pl.ds(0, K - 1)], 1, True)
            wait_out(recv_t.at[pl.ds(0, K - 1)], 1)
            wait_out(send_h.at[pl.ds(0, K - 1)], 11)
        for _ in range(M - 1):
            wait_out(recv_r, 2, True)
            wait_out(recv_t, 2)
            wait_out(recv_g, 13)
        wait_out(pooled.at[pl.ds(0, Z - 1)], 3)

    @pl.when(jnp.logical_not(conc))
    def _():
        wait_out(recv_r.at[pl.ds(0, K)], 1, True)
        wait_out(recv_t.at[pl.ds(0, K)], 1)
        wait_out(send_h, 11)


def local_step(
    dense_input,
    labels,
    table,
    adagrad_state,
    new_owner,
    bag_owner,
    bag_slot,
    bag_offsets,
    bag_length,
    w_first,
    b_first,
    w_out,
):
    blocks = table.shape[0]
    samples = dense_input.shape[0]
    hidden = w_first.shape[1]
    S = Shape(lax.axis_size("dp"), lax.axis_size("mp"), blocks, samples, hidden)
    C, Y, Z, M, K, G, N = S.C, S.Y, S.Z, S.M, S.K, S.G, S.N
    R2 = K * G * 8
    V = pltpu.VMEM
    vmem = pl.BlockSpec(memory_space=pltpu.VMEM)
    hrows = 512 // C
    out_t, out_s, out_w, out_v = pl.pallas_call(
        functools.partial(kernel, S),
        out_shape=(
            jax.ShapeDtypeStruct((blocks * 8, W), F32),
            jax.ShapeDtypeStruct((Y, Z, 4, W), F32),
            jax.ShapeDtypeStruct((512, hidden), BF),
            jax.ShapeDtypeStruct((C, Y, S.V, W), F32),
        ),
        in_specs=[vmem] * 12,
        out_specs=(vmem,) * 4,
        scratch_shapes=[
            V((2 * S.T * 8, W), F32),
            V((G, K, 16, W), BF),
            V((G, K, 1, W), F32),
            V((G, K, 16, W), BF),
            V((G, K, 1, W), F32),
            V((Z, G, 16, W), BF),
            V((Z, G, 1, W), F32),
            V((N, W), F32),
            V((Z, G * 8, W), BF),
            V((K, G * 8, W), BF),
            V((G, K * 8, W), BF),
            V((M, G, K * 8, W), BF),
            V((M, 8, samples), F32),
            V((samples, hidden), F32),
            V((samples, hidden), F32),
            V((4, samples, W), BF),
            V((M, R2, W), BF),
            V((M, R2, W), BF),
            V((G, K * 8, W), BF),
            V((G, K * 8, W), BF),
            V((K, G * 8, W), BF),
            V((Z, G * 8, W), BF),
            V((hrows, hidden), BF),
            V((hrows, hidden), F32),
            V((hrows, hidden), BF),
            V((Y, S.RY, hidden), BF),
            V((hrows, hidden), F32),
            V((Y, S.RY, hidden), BF),
            V((Z, S.pr, S.pc), BF),
            V((Z, S.pr, S.pc), BF),
            V((C, Y, S.V, W), F32),
            V((Y, S.V, W), F32),
            V((Y, S.V, W), F32),
            V((S.V, W), F32),
            V((Z, S.V, W), F32),
            pltpu.SemaphoreType.DMA((16,)),
            pltpu.SemaphoreType.DMA((16,)),
            pltpu.SemaphoreType.DMA((16,)),
            pltpu.SemaphoreType.DMA((16,)),
        ],
        compiler_params=pltpu.CompilerParams(
            collective_id=0, has_side_effects=True, vmem_limit_bytes=56 * 1024 * 1024
        ),
    )(
        new_owner.reshape(1, blocks),
        bag_owner.reshape(1, 3 * samples),
        bag_slot.reshape(1, 3 * samples),
        bag_offsets,
        bag_length.reshape(1, 3 * samples),
        dense_input,
        labels.reshape(1, samples),
        table.reshape(blocks * 8, W),
        adagrad_state,
        w_first,
        b_first.reshape(1, hidden),
        w_out.reshape(1, hidden),
    )
    vecs = out_v.reshape(C, hidden)
    return (
        out_t.reshape(blocks, 8, W),
        out_s.reshape(blocks, W)[:, :8],
        out_w,
        vecs[0],
        vecs[1],
    )


def solution(mesh):
    placed = (
        P("dp", None),
        P("dp"),
        P("dp", None, None),
        P("dp", None),
        P("dp"),
        P("dp", None),
        P("dp"),
        P("dp", None),
        P("dp"),
        P(None, "mp"),
        P("mp"),
        P("mp"),
    )
    return jax.shard_map(
        local_step,
        mesh=mesh,
        in_specs=placed,
        out_specs=(P("dp", None, None), P("dp", None), P(None, "mp"), P("mp"), P("mp")),
        check_vma=False,
    )
```

```python
import functools

import jax
import jax.numpy as jnp
from jax import lax
from jax.experimental import pallas as pl
from jax.experimental.pallas import tpu as pltpu
from jax.sharding import PartitionSpec as P

MESH = pl.DeviceIdType.MESH
BF = jnp.bfloat16
F32 = jnp.float32
I32 = jnp.int32
learn_rate = 0.01
epsilon = 1e-08
W = 128


def iota(shape, dim):
    return lax.broadcasted_iota(I32, shape, dim)


def dot(a, b, dims=((1,), (0,)), exact=False):
    return lax.dot_general(
        a,
        b,
        (dims, ((), ())),
        precision=lax.Precision.HIGHEST if exact else None,
        preferred_element_type=F32,
    )


def log2(n):
    return n.bit_length() - 1


def onehot(mask):
    return jnp.where(mask, 1.0, 0.0).astype(BF)


def to_col(row, rows, pick):
    return jnp.sum(jnp.where(pick, row, 0.0), axis=1, keepdims=True)


class Shape:
    def __init__(self, dp, mp, blocks, samples, hidden):
        self.C = 2
        self.Y = 4 if dp == 128 else 2
        self.Z = dp // (self.C * self.Y)
        self.M = mp
        self.K = self.Z // mp
        self.G = self.Y * self.C
        self.N = dp
        self.NB = blocks
        self.B = samples
        self.HL = hidden
        self.T = self.G * self.K
        self.RY = 512 // (self.C * self.Y)
        self.RG = min(self.Z, self.RY // 16)
        self.CG = self.Z // self.RG
        self.pr = self.RY // self.RG
        self.Q = 2
        self.HQ = hidden // self.Q
        self.pc = self.HQ // self.CG
        self.V = hidden // (W * self.Y)


def kernel(
    S,
    *refs,
):
    given, rest = refs[:12], refs[12:]
    held, inner = rest[-12:], rest[:-12]
    run(S, given, held, *inner)


def run(
    S,
    given,
    held,
    out_t,
    out_d,
    out_s,
    out_w,
    out_v,
    stage_s,
    stage_t,
    send_t,
    send_r,
    mid_t,
    mid_r,
    mid_q,
    recv_t,
    recv_r,
    pooled,
    mid_p,
    send_p,
    slots,
    lbuf,
    act,
    slope,
    feat,
    from_slot,
    to_slot,
    swap_ref,
    inputs,
    part_s,
    recv_x,
    send_h,
    recv_g,
    send_c,
    keep_c,
    recv_c,
    send_y,
    keep_y,
    recv_y,
    send_z,
    recv_z,
    vec,
    vec_c,
    vec_y,
    vec_ys,
    vec_z,
    ss,
    rs,
    sr,
    rr,
    in_sem,
):
    (owner_ref, bown_ref, bslot_ref, boff_ref, blen_ref, dense_ref, label_ref, table_ref, state_ref, w_ref, b_ref, wo_ref) = held
    C, Y, Z, M, K, G, N, NB, B, HL, T = S.C, S.Y, S.Z, S.M, S.K, S.G, S.N, S.NB, S.B, S.HL, S.T
    B3 = 3 * B
    NS = N * 8
    lY, lZ, lM, lK, lG = log2(Y), log2(Z), log2(M), log2(K), log2(G)
    me = lax.axis_index("dp")
    m = lax.axis_index("mp")
    c = lax.rem(me, C)
    z = lax.rem(me // C, Z)
    y = me // (C * Z)
    g = y * C + c
    half = M // 2
    home = lax.rem(z + half * c, M)
    conc = home == m
    base_z = lax.rem(m + M - half * c, M)

    def dp_of(gg, zz):
        return ((gg // C) * Z + zz) * C + lax.rem(gg, C)

    def remote(src, dst, i, dp, mp, small=False):
        pltpu.make_async_remote_copy(
            src_ref=src,
            dst_ref=dst,
            send_sem=(sr if small else ss).at[i],
            recv_sem=(rr if small else rs).at[i],
            device_id=(dp, mp),
            device_id_type=MESH,
        ).start()

    def local(src, dst, i, small=False):
        pltpu.make_async_copy(src, dst, (rr if small else rs).at[i]).start()

    def wait_in(ref, i, small=False):
        pltpu.make_async_copy(ref, ref, (rr if small else rs).at[i]).wait()

    def wait_out(ref, i, small=False):
        pltpu.make_async_copy(ref, ref, (sr if small else ss).at[i]).wait()

    ins = {}
    outs = []

    def take(name):
        ins.pop(name)()

    def sent(ref, i, small=False):
        outs.append(lambda: wait_out(ref, i, small))

    def sent_if(cond, body):
        outs.append(lambda: pl.when(cond)(body))

    def each(lo, hi, body):
        def step(t, carry):
            body(t)
            return carry

        lax.fori_loop(lo, hi, step, 0)

    loads = [pltpu.make_async_copy(a, h, in_sem.at[i]) for i, (a, h) in enumerate(zip(given, held))]
    for load in loads:
        load.start()

    barrier = pltpu.get_barrier_semaphore()

    def greet(dp, mp):
        pl.semaphore_signal(barrier, inc=1, device_id=(dp, mp), device_id_type=MESH)

    ys = [lax.rem(y + i, Y) for i in range(Y)]
    cs = [c, 1 - c]
    ms = [lax.rem(m + i, M) for i in range(M)]
    steps = [(i, j, k) for i in range(Y) for j in range(C) for k in range(M) if (i, j, k) != (0, 0, 0)]
    steps.sort(key=lambda a: -(min(a[0], Y - a[0]) + min(a[2], M - a[2])))
    near = [((ys[i] * Z + z) * C + cs[j], ys[i] * C + cs[j], ms[k]) for i, j, k in steps]

    def along_z(body):
        def step(i):
            away = (i + 1) // 2
            body(lax.rem(z + Z // 2 + Z + away * (1 - 2 * lax.rem(i, 2)), Z))

        each(0, Z - 1, step)

    for dp, _, mm in near:
        greet(dp, mm)
    along_z(lambda zz: greet(dp_of(g, zz), m))

    for load in loads[:9]:
        load.wait()

    def target_of(tt):
        gg = lax.shift_right_logical(tt, lK)
        kk = tt & (K - 1)
        yy = lax.shift_right_logical(gg, 1)
        cc = gg & 1
        zz = ((m + M - half * cc) & (M - 1)) + M * kk
        return (yy * Z + zz) * C + cc

    own_row = owner_ref[...].astype(F32)
    own_col = to_col(own_row, NB, iota((NB, NB), 0) == iota((NB, NB), 1))
    rank_row = jnp.sum(
        jnp.where((own_col == own_row) & (iota((NB, NB), 0) < iota((NB, NB), 1)), 1.0, 0.0),
        axis=0,
        keepdims=True,
    )
    rows2 = iota((2 * T, 1), 0)
    want = target_of(lax.shift_right_logical(rows2, 1)).astype(F32)
    pick_f = jnp.where((own_row == want) & (rank_row == (rows2 & 1).astype(F32)), 1.0, 0.0)
    pick = pick_f.astype(BF)
    for r in range(8):
        low = table_ref[pl.ds(r, NB, stride=8), :].astype(BF)
        stage_t[pl.ds(r, 2 * T, stride=8), :] = dot(pick, low)
    send_t[...] = stage_t[...].astype(BF).reshape(G, K, 16, W)

    bo = bown_ref[...]
    bo_row = bo.astype(F32)
    bo_col = to_col(bo_row, B3, iota((B3, B3), 0) == iota((B3, B3), 1))
    brank_row = jnp.sum(
        jnp.where((bo_col == bo_row) & (iota((B3, B3), 0) < iota((B3, B3), 1)), 1.0, 0.0),
        axis=0,
        keepdims=True,
    )
    slot_nat = bslot_ref[...].reshape(1, B3)
    sy = lax.shift_right_logical(slot_nat, lZ + 2)
    sz = lax.shift_right_logical(slot_nat, 2) & (Z - 1)
    slot_z = ((sz * Y + sy) * 4 + (slot_nat & 3)).astype(F32)
    live = iota((16, B3), 0) < blen_ref[...].reshape(1, B3)
    offs = jnp.where(live, boff_ref[...], -1)
    cnts = [jnp.sum(jnp.where(offs == o, 1.0, 0.0), axis=0, keepdims=True) for o in range(8)]
    line = iota((8, B3), 0)
    cnt8 = jnp.zeros((8, B3), F32)
    for o in range(8):
        cnt8 = jnp.where(line == o, cnts[o], cnt8)
    one16 = jnp.concatenate([cnt8, jnp.where(line == 0, slot_z, 0.0)], axis=0)
    req = jnp.concatenate([one16] * 8, axis=0)
    req = jnp.where(lax.shift_right_logical(iota((W, B3), 0), 4).astype(F32) == brank_row, req, 0.0).astype(BF)
    want_t = target_of(iota((T, 1), 0)).astype(F32)
    rows = dot(onehot(bo_row == want_t), req, ((1,), (1,)))
    for p in range(2):
        pad = [jnp.zeros((96 + 8 * p, NB), F32), state_ref[...], jnp.zeros((24 - 8 * p, NB), F32)]
        pick_p = jnp.where((own_row == want_t) & (rank_row == float(p)), 1.0, 0.0)
        rows = rows + dot(pick_p, jnp.concatenate(pad, axis=0), ((1,), (1,)), exact=True)
    for t in range(T):
        send_r[t // K, t % K] = rows[t : t + 1, :]

    pl.semaphore_wait(barrier, (M * G - 1) + (Z - 1))

    local(send_r.at[g], mid_r.at[g], 0, True)
    local(send_t.at[g], mid_t.at[g], 0)

    def fwd_a(t):
        gg = lax.rem(g + t, G)
        remote(send_r.at[gg], mid_r.at[g], 0, dp_of(gg, z), m, True)
        remote(send_t.at[gg], mid_t.at[g], 0, dp_of(gg, z), m)

    each(1, G, fwd_a)
    sent(mid_r.at[pl.ds(0, G - 1)], 0, True)
    sent(mid_t.at[pl.ds(0, G - 1)], 0)
    ins["mid"] = lambda: (wait_in(mid_r, 0, True), wait_in(mid_t, 0))
    take("mid")
    for t in range(T):
        mid_q[t % K, pl.ds(t // K, 1), :] = mid_r[t // K, t % K]

    def fwd_b(k):
        zz = base_z + M * k

        @pl.when(zz != z)
        def _():
            remote(mid_q.at[k], recv_r.at[z], 1, dp_of(g, zz), m, True)
            remote(mid_t.at[:, k], recv_t.at[z], 1, dp_of(g, zz), m)

        @pl.when(zz == z)
        def _():
            local(mid_q.at[k], recv_r.at[z], 1, True)
            local(mid_t.at[:, k], recv_t.at[z], 1)

    each(0, K, fwd_b)

    def fwd_b_sent(n):
        if n:
            wait_out(recv_r.at[pl.ds(0, n)], 1, True)
            wait_out(recv_t.at[pl.ds(0, n)], 1)

    sent_if(conc, lambda: fwd_b_sent(K - 1))
    sent_if(jnp.logical_not(conc), lambda: fwd_b_sent(K))

    def wait_blocks():
        wait_in(recv_r, 1, True)
        wait_in(recv_t, 1)

    ins["blocks"] = lambda: pl.when(conc)(wait_blocks)

    oc = bo & 1
    oz = lax.shift_right_logical(bo, 1) & (Z - 1)
    oy = lax.shift_right_logical(bo, 1 + lZ)
    om = (oz + half * oc) & (M - 1)
    ok = lax.shift_right_logical(oz, lM)
    place = (((om * G + oy * C + oc) * K + ok) * 8).astype(F32) + brank_row
    pcol, prow = [], []
    for f in range(3):
        col = to_col(place, B, iota((B, B3), 1) == 3 * iota((B, B3), 0) + f)
        pcol.append(col)
        prow.append(jnp.sum(jnp.where(iota((B, B), 0) == iota((B, B), 1), col, 0.0), axis=0, keepdims=True))

    low16 = iota((W, W), 0) & 15
    tile_c = onehot(low16 == (iota((W, W), 1) & 7))
    tile_s = onehot(low16 == 8)

    CH = min(NS, 2 * G * 8)

    def entries(i, n):
        row = iota((n, N), 0) + i * n
        src = onehot(lax.shift_right_logical(row, 3) == iota((n, N), 1))
        wide = dot(src, jnp.where(iota((N, W), 1) < 96, recv_r[...].reshape(N, W), 0.0).astype(BF))
        keep = lax.shift_right_logical(iota((n, W), 1), 4) == (iota((n, W), 0) & 7)
        return jnp.where(keep, wide, 0.0).astype(BF)

    R2 = K * G * 8
    ro = iota((R2, R2), 0)
    ri = iota((R2, R2), 1)
    for i, (a, b) in enumerate(((ro, ri), (ri, ro))):
        swap_ref[i] = onehot(
            (lax.shift_right_logical(a, lK + 3) == (lax.shift_right_logical(b, 3) & (G - 1)))
            & ((lax.shift_right_logical(a, 3) & (K - 1)) == lax.shift_right_logical(b, lG + 3))
            & ((a & 7) == (b & 7))
        )
    for f in range(3):
        from_slot[f] = onehot(iota((B, NS), 1).astype(F32) == pcol[f])
        for q in range(M):
            to_slot[q, :, f * B : (f + 1) * B] = onehot((iota((R2, B), 0) + q * R2).astype(F32) == prow[f])

    take("blocks")

    def cast_r():
        each(1, M, lambda t: remote(recv_r, recv_r, 2, me, lax.rem(m + t, M), True))

    def cast_r_sent():
        for _ in range(M - 1):
            wait_out(recv_r, 2, True)

    pl.when(conc)(cast_r)
    sent_if(conc, cast_r_sent)
    ins["cast_r"] = lambda: pl.when(jnp.logical_not(conc))(lambda: wait_in(recv_r, 2, True))

    @pl.when(conc)
    def _():
        def pool(step):
            n = NS // CH
            away = (step + 1) // 2
            i = lax.rem(z // (Z // n) + n // 2 + n + away * (1 - 2 * lax.rem(step, 2)), n)
            ent = entries(i, CH)
            cnt = dot(ent, tile_c)
            slt = dot(ent, tile_s)
            group = lax.shift_right_logical(iota((CH, W), 1), 3)
            parts = [
                jnp.where(slt == (group + 16 * q).astype(F32), cnt, 0.0).astype(BF) for q in range(NB // 16)
            ]
            wide = jnp.concatenate(parts, axis=1) if len(parts) > 1 else parts[0]
            got = dot(wide, recv_t[...].reshape(NB * 8, W))
            per = CH // (G * 8)
            pooled[pl.ds(i * per, per)] = got.astype(BF).reshape(per, G * 8, W)

            def send(q):
                zz = i * per + q

                @pl.when(zz != z)
                def _():
                    remote(pooled.at[zz], mid_p.at[z // M], 3, dp_of(g, zz), m)

                @pl.when(zz == z)
                def _():
                    local(pooled.at[zz], mid_p.at[z // M], 3)

            each(0, per, send)

        each(0, NS // CH, pool)

    sent_if(conc, lambda: wait_out(pooled.at[pl.ds(0, Z - 1)], 3))
    ins["pooled"] = lambda: wait_in(mid_p, 3)

    take("pooled")
    send_p[...] = dot(swap_ref[0], mid_p[...].reshape(R2, W)).astype(BF).reshape(G, K * 8, W)
    local(send_p.at[g], slots.at[m * G + g], 4)

    for dp, gg, mm in near:
        remote(send_p.at[gg], slots.at[m * G + g], 4, dp, mm)
    sent(slots.at[pl.ds(0, M * G - 1)], 4)
    ins["slots"] = lambda: wait_in(slots, 4)
    take("slots")

    for load in loads[9:]:
        load.wait()
    table_s = slots[...].reshape(NS, W)
    feat[0] = dense_ref[...]
    for f in range(3):
        feat[f + 1] = dot(from_slot[f], table_s).astype(BF)
    features = jnp.concatenate([feat[i] for i in range(4)], axis=1)
    pre = dot(features, w_ref[...]) + b_ref[...]
    sig = jax.nn.sigmoid(pre)
    active = pre * sig
    act[...] = active
    slope[...] = sig * (1.0 + pre * (1.0 - sig)) * wo_ref[...]
    part = jnp.sum(active * wo_ref[...], axis=1, keepdims=True)
    eye_b = iota((B, B), 0) == iota((B, B), 1)
    part_row = jnp.sum(jnp.where(eye_b, part, 0.0), axis=0, keepdims=True)
    lbuf[m] = jnp.broadcast_to(part_row, (8, B))
    each(1, M, lambda t: remote(lbuf.at[m], lbuf.at[m], 3, me, lax.rem(m + t, M), True))
    sent(lbuf.at[pl.ds(0, M - 1)], 3, True)
    ins["logits"] = lambda: wait_in(lbuf.at[pl.ds(0, M - 1)], 3, True)
    take("logits")

    total = lbuf[0]
    for i in range(1, M):
        total = total + lbuf[i]
    lgrad_row = jax.nn.sigmoid(total[0:1, :]) - label_ref[...].astype(F32)
    lgrad = to_col(lgrad_row, B, eye_b)
    grad_pre = lgrad * slope[...]
    grad_low = grad_pre.astype(BF)
    hrows = 512 // C
    other = 1 - c
    mate = me + 1 - 2 * c

    def term_of(i, blk):
        return dot(feat[i], blk, ((0,), (0,)))

    for q in range(S.Q):
        low_q = grad_low[:, q * S.HQ : (q + 1) * S.HQ]
        for h in range(C):

            @pl.when(c != h)
            def _():
                for i in range(2):
                    send_c[q, pl.ds(i * W, W), :] = term_of(2 * h + i, low_q).astype(BF)

            @pl.when(c == h)
            def _():
                for i in range(2):
                    keep_c[q, pl.ds(i * W, W), :] = term_of(2 * h + i, low_q)

        remote(send_c.at[q], recv_c.at[q], 16 + q, mate, m)
        sent(send_c.at[q], 16 + q)
        ins["core", q] = lambda q=q: wait_in(recv_c.at[q], 16 + q)

    for f in range(3):
        term = dot(grad_low, w_ref[pl.ds((f + 1) * W, W), :], ((1,), (1,)))
        inputs[pl.ds(f * B, B), :] = term.astype(BF)
    for q in range(S.Q):
        take(("core", q))
        keep_y[q] = keep_c[q] + recv_c[q].astype(F32)
        send_y[q] = keep_y[q].astype(BF).reshape(Y, S.RY, S.HQ)

        def to_y(t):
            yy = lax.rem(y + t, Y)
            remote(send_y.at[q, yy], recv_y.at[q, y], 18 + q, (yy * Z + z) * C + c, m)

        each(1, Y, to_y)
        sent(send_y.at[q, pl.ds(0, Y - 1)], 18 + q)
        ins["dense_y", q] = lambda q=q: wait_in(recv_y.at[q, pl.ds(0, Y - 1)], 18 + q)
    for q in range(M):
        part_s[q] = dot(to_slot[q], inputs[...]).astype(BF).reshape(G, K * 8, W)

    local(part_s.at[m, g], recv_x.at[m * G + g], 7)
    for dp, gg, mm in near:
        remote(part_s.at[mm, gg], recv_x.at[m * G + g], 7, dp, mm)
    sent(recv_x.at[pl.ds(0, M * G - 1)], 7)
    ins["bags_x"] = lambda: wait_in(recv_x, 7)

    b1 = jnp.sum(grad_pre, axis=0, keepdims=True)
    w2 = jnp.sum(lgrad * act[...], axis=0, keepdims=True)
    for i, row in enumerate((b1, w2)):
        for j in range(HL // W):
            vec[i, j // S.V, pl.ds(j % S.V, 1), :] = row[:, j * W : (j + 1) * W]

    remote(vec.at[other], vec_c, 6, mate, m, True)
    sent(vec_c, 6, True)
    ins["core_v"] = lambda: wait_in(vec_c, 6, True)


    take("core_v")
    vec[c] = vec[c] + vec_c[...]

    def to_y_vec(t):
        yy = lax.rem(y + t, Y)
        remote(vec.at[c, yy], vec_y.at[y], 8, (yy * Z + z) * C + c, m, True)

    each(1, Y, to_y_vec)
    sent(vec_y.at[pl.ds(0, Y - 1)], 8, True)
    ins["dense_yv"] = lambda: wait_in(vec_y.at[pl.ds(0, Y - 1)], 8, True)

    def dense_z(q):
        take(("dense_y", q))
        acc = keep_y[q, pl.ds(pl.multiple_of(y * S.RY, S.RY), S.RY), :]
        for t in range(1, Y):
            acc = acc + recv_y[q, lax.rem(y + t, Y)].astype(F32)
        for i in range(Z):
            r0, c0 = (i // S.CG) * S.pr, (i % S.CG) * S.pc
            send_z[q, i] = acc[r0 : r0 + S.pr, c0 : c0 + S.pc].astype(BF)
        local(send_z.at[q, z], recv_z.at[q, z], 20 + q)

        def to_z(zz):
            remote(send_z.at[q, zz], recv_z.at[q, z], 20 + q, dp_of(g, zz), m)

        along_z(to_z)
        sent(send_z.at[q, pl.ds(0, Z - 1)], 20 + q)
        ins["dense_z", q] = lambda: wait_in(recv_z.at[q], 20 + q)

    for q in range(S.Q):
        dense_z(q)

    take("bags_x")
    total = recv_x[pl.ds(0, G)].astype(F32)
    for i in range(1, M):
        total = total + recv_x[pl.ds(i * G, G)].astype(F32)
    send_h[...] = dot(swap_ref[1], total.astype(BF).reshape(R2, W)).astype(BF).reshape(K, G * 8, W)

    def grad_b(k):
        zz = base_z + M * k

        @pl.when(zz != z)
        def _():
            remote(send_h.at[k], recv_g.at[z], 11, dp_of(g, zz), m)

        @pl.when(zz == z)
        def _():
            local(send_h.at[k], recv_g.at[z], 11)

    each(0, K, grad_b)

    def grad_b_sent(n):
        if n:
            wait_out(send_h.at[pl.ds(0, n)], 11)

    sent_if(conc, lambda: grad_b_sent(K - 1))
    sent_if(jnp.logical_not(conc), lambda: grad_b_sent(K))
    ins["grads"] = lambda: pl.when(conc)(lambda: wait_in(recv_g, 11))


    take("dense_yv")
    accv = vec[c, y]
    for t in range(1, Y):
        accv = accv + vec_y[lax.rem(y + t, Y)]
    vec_ys[...] = accv
    local(vec_ys, vec_z.at[z], 10, True)
    along_z(lambda zz: remote(vec_ys, vec_z.at[z], 10, dp_of(g, zz), m, True))
    sent(vec_z.at[pl.ds(0, Z - 1)], 10, True)
    ins["dense_zv"] = lambda: wait_in(vec_z, 10, True)
    def cast_t():
        for h in range(2):
            part = recv_t.at[pl.ds(h * (Z // 2), Z // 2)]
            each(1, M, lambda t: remote(part, part, 2, me, lax.rem(m + t, M)))

    def cast_t_sent():
        for _ in range(M - 1):
            wait_out(recv_t, 2)

    pl.when(conc)(cast_t)
    sent_if(conc, cast_t_sent)
    ins["cast_t"] = lambda: pl.when(jnp.logical_not(conc))(lambda: wait_in(recv_t, 2))


    block0 = c * hrows + y * S.RY

    def gather_z(q):
        take(("dense_z", q))

        def add_z(i, carry):
            return carry + recv_z[q, i].astype(F32)

        acc = lax.fori_loop(0, Z, add_z, jnp.zeros((S.pr, S.pc), F32))
        r0 = pl.multiple_of(block0 + (z // S.CG) * S.pr, 16)
        c0 = pl.multiple_of(q * S.HQ + lax.rem(z, S.CG) * S.pc, W)
        out_w[pl.ds(r0, S.pr), pl.ds(c0, S.pc)] = acc.astype(BF)
        piece = out_w.at[pl.ds(r0, S.pr), pl.ds(c0, S.pc)]
        along_z(lambda zz: remote(piece, piece, 22 + q, dp_of(g, zz), m))
        sent(send_z.at[q, pl.ds(0, Z - 1)], 22 + q)
        ins["out_z", q] = lambda: wait_in(send_z.at[q, pl.ds(0, Z - 1)], 22 + q)


    for q in range(S.Q):
        gather_z(q)
    take("cast_r")
    sel = onehot((iota((16, W), 1) & 15) == iota((16, W), 0))
    lists = dot(sel, entries(0, NS), ((1,), (1,)))
    list8 = lists[0:8, :]
    slot_row = lists[8:9, :]
    take("grads")

    @pl.when(conc)
    def _():
        each(1, M, lambda t: remote(recv_g, recv_g, 13, me, lax.rem(m + t, M)))

    def grads_sent():
        for _ in range(M - 1):
            wait_out(recv_g, 13)

    sent_if(conc, grads_sent)
    ins["grads_x"] = lambda: pl.when(jnp.logical_not(conc))(lambda: wait_in(recv_g, 13))

    take("dense_zv")
    accv = vec_z[0]
    for i in range(1, Z):
        accv = accv + vec_z[i]
    out_v[c, y] = accv

    def ag_yv(t):
        yy = lax.rem(y + t, Y)
        remote(out_v.at[c, y], out_v.at[c, y], 14, (yy * Z + z) * C + c, m, True)

    each(1, Y, ag_yv)
    sent(out_v.at[0, pl.ds(0, Y - 1)], 14, True)
    ins["out_yv"] = lambda: wait_in(out_v.at[0, pl.ds(0, Y - 1)], 14, True)

    QR = G * 16

    def update(pair):
        for i in (2 * pair, 2 * pair + 1):
            update_one(i)

    def update_one(i):
        row = iota((QR, 1), 0)
        slot_id = (lax.shift_right_logical(row, 3) + i * (QR // 8)).astype(F32)
        cnt = jnp.broadcast_to(list8[None], (QR // 8, 8, NS)).reshape(QR, NS)
        wide = jnp.where(slot_row == slot_id, cnt, 0.0).astype(BF)
        grad = dot(wide, recv_g[...].reshape(NS, W))
        src_rows = recv_r[i]
        wide_s = jnp.broadcast_to(src_rows[:, None, :], (G, 16, W)).reshape(QR, W)
        pick_s = iota((QR, W), 1) == (iota((QR, W), 0) & 15) + 96
        st = jnp.sum(jnp.where(pick_s, wide_s, 0.0), axis=1, keepdims=True)
        st = st + jnp.sum(grad * grad, axis=1, keepdims=True) * (1.0 / W)
        low = recv_t[i].reshape(QR, W)
        step = (learn_rate * grad / (jnp.sqrt(st) + epsilon)).astype(BF)
        pick_o = iota((QR, W), 1) == (iota((QR, W), 0) & 7)
        st8 = jnp.sum(jnp.where(pick_o, st, 0.0).reshape(QR // 8, 8, W), axis=1)
        for q in range(Y):
            at = pl.ds(pl.multiple_of((q * Z + i) * 32, 32), 32)
            out_t[at, :] = low[q * 32 : (q + 1) * 32]
            out_d[at, :] = step[q * 32 : (q + 1) * 32]
            stage_s[pl.ds((q * Z + i) * 4, 4), :] = st8[q * 4 : (q + 1) * 4]

    for q in range(S.Q):
        take(("out_z", q))
        mine = out_w.at[pl.ds(pl.multiple_of(block0, 16), S.RY), pl.ds(q * S.HQ, S.HQ)]

        def ag_y(t):
            yy = lax.rem(y + t, Y)
            remote(mine, mine, 24 + q, (yy * Z + z) * C + c, m)

        each(1, Y, ag_y)
        sent(send_y.at[q, pl.ds(0, Y - 1)], 24 + q)
        ins["out_y", q] = lambda q=q: wait_in(send_y.at[q, pl.ds(0, Y - 1)], 24 + q)

    take("cast_t")
    take("grads_x")
    each(0, Z // 2, update)

    def gather_core(q):
        take(("out_y", q))
        part = out_w.at[pl.ds(pl.multiple_of(c * hrows, 16), hrows), pl.ds(q * S.HQ, S.HQ)]
        remote(part, part, 26 + q, mate, m)
        sent(send_c.at[q], 26 + q)
        ins["out_c", q] = lambda: wait_in(recv_c.at[q], 26 + q)

    for q in range(S.Q):
        gather_core(q)
    take("out_yv")
    remote(out_v.at[c], out_v.at[c], 15, mate, m, True)
    sent(vec_c, 15, True)
    ins["out_cv"] = lambda: wait_in(vec_c, 15, True)
    out_s[...] = jnp.transpose(stage_s[...])[0:8, :]
    take("out_cv")
    for q in range(S.Q):
        take(("out_c", q))
    assert not ins

    for done in outs:
        done()


def local_step(
    dense_input,
    labels,
    table,
    adagrad_state,
    new_owner,
    bag_owner,
    bag_slot,
    bag_offsets,
    bag_length,
    w_first,
    b_first,
    w_out,
):
    blocks = table.shape[0]
    samples = dense_input.shape[0]
    hidden = w_first.shape[1]
    S = Shape(lax.axis_size("dp"), lax.axis_size("mp"), blocks, samples, hidden)
    C, Y, Z, M, K, G, N = S.C, S.Y, S.Z, S.M, S.K, S.G, S.N
    R2 = K * G * 8
    V = pltpu.VMEM
    vmem = pl.BlockSpec(memory_space=pltpu.VMEM)
    hrows = 512 // C
    args = (
        new_owner.reshape(1, blocks),
        bag_owner.reshape(1, 3 * samples),
        bag_slot,
        bag_offsets.T,
        bag_length,
        dense_input,
        labels.reshape(1, samples),
        table.reshape(blocks * 8, W),
        adagrad_state.T,
        w_first,
        b_first.reshape(1, hidden),
        w_out.reshape(1, hidden),
    )
    out_t, out_d, out_s, out_w, out_v = pl.pallas_call(
        functools.partial(kernel, S),
        out_shape=(
            jax.ShapeDtypeStruct((blocks * 8, W), BF),
            jax.ShapeDtypeStruct((blocks * 8, W), BF),
            jax.ShapeDtypeStruct((8, blocks), F32),
            jax.ShapeDtypeStruct((512, hidden), BF),
            jax.ShapeDtypeStruct((C, Y, S.V, W), F32),
        ),
        in_specs=[pl.BlockSpec(memory_space=pltpu.HBM)] * 12,
        out_specs=(vmem,) * 5,
        scratch_shapes=[
            V((blocks, W), F32),
            V((2 * S.T * 8, W), F32),
            V((G, K, 16, W), BF),
            V((G, K, 1, W), F32),
            V((G, K, 16, W), BF),
            V((G, K, 1, W), F32),
            V((K, G, W), F32),
            V((Z, G, 16, W), BF),
            V((Z, G, W), F32),
            V((Z, G * 8, W), BF),
            V((K, G * 8, W), BF),
            V((G, K * 8, W), BF),
            V((M * G, K * 8, W), BF),
            V((M, 8, samples), F32),
            V((samples, hidden), F32),
            V((samples, hidden), F32),
            V((4, samples, W), BF),
            V((3, samples, S.N * 8), BF),
            V((M, R2, 3 * samples), BF),
            V((2, R2, R2), BF),
            V((3 * samples, W), BF),
            V((M, G, K * 8, W), BF),
            V((M * G, K * 8, W), BF),
            V((K, G * 8, W), BF),
            V((Z, G * 8, W), BF),
            V((S.Q, hrows, S.HQ), BF),
            V((S.Q, hrows, S.HQ), F32),
            V((S.Q, hrows, S.HQ), BF),
            V((S.Q, Y, S.RY, S.HQ), BF),
            V((S.Q, hrows, S.HQ), F32),
            V((S.Q, Y, S.RY, S.HQ), BF),
            V((S.Q, Z, S.pr, S.pc), BF),
            V((S.Q, Z, S.pr, S.pc), BF),
            V((C, Y, S.V, W), F32),
            V((Y, S.V, W), F32),
            V((Y, S.V, W), F32),
            V((S.V, W), F32),
            V((Z, S.V, W), F32),
            pltpu.SemaphoreType.DMA((32,)),
            pltpu.SemaphoreType.DMA((32,)),
            pltpu.SemaphoreType.DMA((32,)),
            pltpu.SemaphoreType.DMA((32,)),
            pltpu.SemaphoreType.DMA((12,)),
        ]
        + [V(a.shape, a.dtype) for a in args],
        compiler_params=pltpu.CompilerParams(
            collective_id=0, has_side_effects=True, vmem_limit_bytes=56 * 1024 * 1024
        ),
    )(*args)
    vecs = out_v.reshape(C, hidden)
    return (
        (out_t.astype(F32) - out_d.astype(F32)).reshape(blocks, 8, W),
        out_s.T,
        out_w,
        vecs[0],
        vecs[1],
    )


def solution(mesh):
    placed = (
        P("dp", None),
        P("dp"),
        P("dp", None, None),
        P("dp", None),
        P("dp"),
        P("dp", None),
        P("dp"),
        P("dp", None),
        P("dp"),
        P(None, "mp"),
        P("mp"),
        P("mp"),
    )
    return jax.shard_map(
        local_step,
        mesh=mesh,
        in_specs=placed,
        out_specs=(P("dp", None, None), P("dp", None), P(None, "mp"), P("mp"), P("mp")),
        check_vma=False,
    )
```

```python
import functools

import jax
import jax.numpy as jnp
from jax import lax
from jax.experimental import pallas as pl
from jax.experimental.pallas import tpu as pltpu
from jax.sharding import PartitionSpec as P

MESH = pl.DeviceIdType.MESH
BF = jnp.bfloat16
F32 = jnp.float32
I32 = jnp.int32
learn_rate = 0.01
epsilon = 1e-08
W = 128


def iota(shape, dim):
    return lax.broadcasted_iota(I32, shape, dim)


def dot(a, b, dims=((1,), (0,)), exact=False):
    return lax.dot_general(
        a,
        b,
        (dims, ((), ())),
        precision=lax.Precision.HIGHEST if exact else None,
        preferred_element_type=F32,
    )


def log2(n):
    return n.bit_length() - 1


def onehot(mask):
    return jnp.where(mask, 1.0, 0.0).astype(BF)


def to_col(row, rows, pick):
    return jnp.sum(jnp.where(pick, row, 0.0), axis=1, keepdims=True)


class Shape:
    def __init__(self, dp, mp, blocks, samples, hidden):
        self.C = 2
        self.Y = 4 if dp == 128 else 2
        self.Z = dp // (self.C * self.Y)
        self.M = mp
        self.K = self.Z // mp
        self.G = self.Y * self.C
        self.N = dp
        self.NB = blocks
        self.B = samples
        self.HL = hidden
        self.T = self.G * self.K
        self.RY = 512 // (self.C * self.Y)
        self.RG = min(self.Z, self.RY // 16)
        self.CG = self.Z // self.RG
        self.pr = self.RY // self.RG
        self.Q = 2
        self.HQ = hidden // self.Q
        self.pc = self.HQ // self.CG
        self.V = hidden // (W * self.Y)


def kernel(
    S,
    *refs,
):
    given, results, rest = refs[:12], refs[12:17], refs[17:]
    held, made, inner = rest[-17:-5], rest[-5:], rest[:-17]
    run(S, given, held, results, *made, *inner)


def run(
    S,
    given,
    held,
    results,
    out_t,
    out_d,
    out_s,
    out_w,
    out_v,
    stage_s,
    stage_t,
    send_t,
    send_r,
    mid_t,
    mid_r,
    mid_q,
    recv_t,
    recv_r,
    pooled,
    mid_p,
    send_p,
    slots,
    lbuf,
    act,
    slope,
    feat,
    feat_t,
    from_slot,
    to_slot,
    swap_ref,
    inputs,
    part_s,
    recv_x,
    send_h,
    recv_g,
    send_c,
    keep_c,
    recv_c,
    send_y,
    keep_y,
    recv_y,
    send_z,
    recv_z,
    vec,
    vec_c,
    vec_y,
    vec_ys,
    vec_z,
    ss,
    rs,
    sr,
    rr,
    in_sem,
    out_sem,
):
    (owner_ref, bown_ref, bslot_ref, boff_ref, blen_ref, dense_ref, label_ref, table_ref, state_ref, w_ref, b_ref, wo_ref) = held
    C, Y, Z, M, K, G, N, NB, B, HL, T = S.C, S.Y, S.Z, S.M, S.K, S.G, S.N, S.NB, S.B, S.HL, S.T
    B3 = 3 * B
    NS = N * 8
    lY, lZ, lM, lK, lG = log2(Y), log2(Z), log2(M), log2(K), log2(G)
    me = lax.axis_index("dp")
    m = lax.axis_index("mp")
    c = lax.rem(me, C)
    z = lax.rem(me // C, Z)
    y = me // (C * Z)
    g = y * C + c
    half = M // 2
    home = lax.rem(z + half * c, M)
    conc = home == m
    base_z = lax.rem(m + M - half * c, M)

    def dp_of(gg, zz):
        return ((gg // C) * Z + zz) * C + lax.rem(gg, C)

    def remote(src, dst, i, dp, mp, small=False):
        pltpu.make_async_remote_copy(
            src_ref=src,
            dst_ref=dst,
            send_sem=(sr if small else ss).at[i],
            recv_sem=(rr if small else rs).at[i],
            device_id=(dp, mp),
            device_id_type=MESH,
        ).start()

    def local(src, dst, i, small=False):
        pltpu.make_async_copy(src, dst, (rr if small else rs).at[i]).start()

    def wait_in(ref, i, small=False):
        pltpu.make_async_copy(ref, ref, (rr if small else rs).at[i]).wait()

    def wait_out(ref, i, small=False):
        pltpu.make_async_copy(ref, ref, (sr if small else ss).at[i]).wait()

    ins = {}
    outs = []

    def take(name):
        ins.pop(name)()

    def sent(ref, i, small=False):
        outs.append(lambda: wait_out(ref, i, small))

    def sent_if(cond, body):
        outs.append(lambda: pl.when(cond)(body))

    def each(lo, hi, body):
        def step(t, carry):
            body(t)
            return carry

        lax.fori_loop(lo, hi, step, 0)

    barrier = pltpu.get_barrier_semaphore()

    def greet(dp, mp):
        pl.semaphore_signal(barrier, inc=1, device_id=(dp, mp), device_id_type=MESH)

    ys = [lax.rem(y + i, Y) for i in range(Y)]
    cs = [c, 1 - c]
    ms = [lax.rem(m + i, M) for i in range(M)]
    steps = [(i, j, k) for i in range(Y) for j in range(C) for k in range(M) if (i, j, k) != (0, 0, 0)]
    steps.sort(key=lambda a: -(min(a[0], Y - a[0]) + min(a[2], M - a[2])))
    near = [((ys[i] * Z + z) * C + cs[j], ys[i] * C + cs[j], ms[k]) for i, j, k in steps]

    def along_z(body):
        def step(i):
            away = (i + 1) // 2
            body(lax.rem(z + Z // 2 + Z + away * (1 - 2 * lax.rem(i, 2)), Z))

        each(0, Z - 1, step)

    along_z(lambda zz: greet(dp_of(g, zz), m))
    loads = [pltpu.make_async_copy(a, h, in_sem.at[i]) for i, (a, h) in enumerate(zip(given, held))]
    for load in loads:
        load.start()
    for dp, _, mm in near:
        greet(dp, mm)

    for i in (0, 7):
        loads[i].wait()

    def target_of(tt):
        gg = lax.shift_right_logical(tt, lK)
        kk = tt & (K - 1)
        yy = lax.shift_right_logical(gg, 1)
        cc = gg & 1
        zz = ((m + M - half * cc) & (M - 1)) + M * kk
        return (yy * Z + zz) * C + cc

    own_row = owner_ref[...].astype(F32)
    own_col = to_col(own_row, NB, iota((NB, NB), 0) == iota((NB, NB), 1))
    rank_row = jnp.sum(
        jnp.where((own_col == own_row) & (iota((NB, NB), 0) < iota((NB, NB), 1)), 1.0, 0.0),
        axis=0,
        keepdims=True,
    )
    rows2 = iota((2 * T, 1), 0)
    want = target_of(lax.shift_right_logical(rows2, 1)).astype(F32)
    pick_f = jnp.where((own_row == want) & (rank_row == (rows2 & 1).astype(F32)), 1.0, 0.0)
    pick = pick_f.astype(BF)
    for r in range(8):
        low = table_ref[pl.ds(r, NB, stride=8), :].astype(BF)
        stage_t[pl.ds(r, 2 * T, stride=8), :] = dot(pick, low)
    send_t[...] = stage_t[...].astype(BF).reshape(G, K, 16, W)

    pl.semaphore_wait(barrier, (M * G - 1) + (Z - 1))

    local(send_t.at[g], mid_t.at[g], 0)
    group = [(dp, gg) for (dp, gg, _), (_, _, k) in zip(near, steps) if k == 0]
    for dp, gg in group:
        remote(send_t.at[gg], mid_t.at[g], 0, dp, m)
    sent(mid_t.at[pl.ds(0, G - 1)], 0)
    ins["mid_t"] = lambda: wait_in(mid_t, 0)

    for i in (1, 2, 3, 4, 8):
        loads[i].wait()
    bo = bown_ref[...]
    bo_row = bo.astype(F32)
    bo_col = to_col(bo_row, B3, iota((B3, B3), 0) == iota((B3, B3), 1))
    brank_row = jnp.sum(
        jnp.where((bo_col == bo_row) & (iota((B3, B3), 0) < iota((B3, B3), 1)), 1.0, 0.0),
        axis=0,
        keepdims=True,
    )
    slot_nat = bslot_ref[...].reshape(1, B3)
    sy = lax.shift_right_logical(slot_nat, lZ + 2)
    sz = lax.shift_right_logical(slot_nat, 2) & (Z - 1)
    slot_z = ((sz * Y + sy) * 4 + (slot_nat & 3)).astype(F32)
    live = iota((16, B3), 0) < blen_ref[...].reshape(1, B3)
    offs = jnp.where(live, boff_ref[...], -1)
    cnts = [jnp.sum(jnp.where(offs == o, 1.0, 0.0), axis=0, keepdims=True) for o in range(8)]
    line = iota((8, B3), 0)
    cnt8 = jnp.zeros((8, B3), F32)
    for o in range(8):
        cnt8 = jnp.where(line == o, cnts[o], cnt8)
    one16 = jnp.concatenate([cnt8, jnp.where(line == 0, slot_z, 0.0)], axis=0)
    req = jnp.concatenate([one16] * 8, axis=0)
    req = jnp.where(lax.shift_right_logical(iota((W, B3), 0), 4).astype(F32) == brank_row, req, 0.0).astype(BF)
    want_t = target_of(iota((T, 1), 0)).astype(F32)
    rows = dot(onehot(bo_row == want_t), req, ((1,), (1,)))
    for p in range(2):
        pad = [jnp.zeros((96 + 8 * p, NB), F32), state_ref[...], jnp.zeros((24 - 8 * p, NB), F32)]
        pick_p = jnp.where((own_row == want_t) & (rank_row == float(p)), 1.0, 0.0)
        rows = rows + dot(pick_p, jnp.concatenate(pad, axis=0), ((1,), (1,)), exact=True)
    for t in range(T):
        send_r[t // K, t % K] = rows[t : t + 1, :]

    local(send_r.at[g], mid_r.at[g], 0, True)
    for dp, gg in group:
        remote(send_r.at[gg], mid_r.at[g], 0, dp, m, True)
    sent(mid_r.at[pl.ds(0, G - 1)], 0, True)
    ins["mid_r"] = lambda: wait_in(mid_r, 0, True)

    def fwd_b(mid, recv, small):
        def to(k):
            zz = base_z + M * k

            @pl.when(zz != z)
            def _():
                remote(mid(k), recv.at[z], 1, dp_of(g, zz), m, small)

            @pl.when(zz == z)
            def _():
                local(mid(k), recv.at[z], 1, small)

        each(0, K, to)

    take("mid_t")
    fwd_b(lambda k: mid_t.at[:, k], recv_t, False)
    take("mid_r")
    for t in range(T):
        mid_q[t % K, pl.ds(t // K, 1), :] = mid_r[t // K, t % K]
    fwd_b(lambda k: mid_q.at[k], recv_r, True)

    def fwd_b_sent(n):
        if n:
            wait_out(recv_r.at[pl.ds(0, n)], 1, True)
            wait_out(recv_t.at[pl.ds(0, n)], 1)

    sent_if(conc, lambda: fwd_b_sent(K - 1))
    sent_if(jnp.logical_not(conc), lambda: fwd_b_sent(K))

    def wait_blocks():
        wait_in(recv_r, 1, True)
        wait_in(recv_t, 1)

    ins["blocks"] = lambda: pl.when(conc)(wait_blocks)

    oc = bo & 1
    oz = lax.shift_right_logical(bo, 1) & (Z - 1)
    oy = lax.shift_right_logical(bo, 1 + lZ)
    om = (oz + half * oc) & (M - 1)
    ok = lax.shift_right_logical(oz, lM)
    place = (((om * G + oy * C + oc) * K + ok) * 8).astype(F32) + brank_row
    pcol, prow = [], []
    for f in range(3):
        col = to_col(place, B, iota((B, B3), 1) == 3 * iota((B, B3), 0) + f)
        pcol.append(col)
        prow.append(jnp.sum(jnp.where(iota((B, B), 0) == iota((B, B), 1), col, 0.0), axis=0, keepdims=True))

    low16 = iota((W, W), 0) & 15
    tile_c = onehot(low16 == (iota((W, W), 1) & 7))
    tile_s = onehot(low16 == 8)

    CH = min(NS, 2 * G * 8)

    def entries(i, n):
        row = iota((n, N), 0) + i * n
        src = onehot(lax.shift_right_logical(row, 3) == iota((n, N), 1))
        wide = dot(src, jnp.where(iota((N, W), 1) < 96, recv_r[...].reshape(N, W), 0.0).astype(BF))
        keep = lax.shift_right_logical(iota((n, W), 1), 4) == (iota((n, W), 0) & 7)
        return jnp.where(keep, wide, 0.0).astype(BF)

    R2 = K * G * 8
    ro = iota((R2, R2), 0)
    ri = iota((R2, R2), 1)
    for i, (a, b) in enumerate(((ro, ri), (ri, ro))):
        swap_ref[i] = onehot(
            (lax.shift_right_logical(a, lK + 3) == (lax.shift_right_logical(b, 3) & (G - 1)))
            & ((lax.shift_right_logical(a, 3) & (K - 1)) == lax.shift_right_logical(b, lG + 3))
            & ((a & 7) == (b & 7))
        )
    for f in range(3):
        from_slot[f] = onehot(iota((B, NS), 1).astype(F32) == pcol[f])
        for q in range(M):
            to_slot[q, :, f * B : (f + 1) * B] = onehot((iota((R2, B), 0) + q * R2).astype(F32) == prow[f])

    take("blocks")

    def cast_r():
        each(1, M, lambda t: remote(recv_r, recv_r, 2, me, lax.rem(m + t, M), True))

    def cast_r_sent():
        for _ in range(M - 1):
            wait_out(recv_r, 2, True)

    pl.when(conc)(cast_r)
    sent_if(conc, cast_r_sent)
    ins["cast_r"] = lambda: pl.when(jnp.logical_not(conc))(lambda: wait_in(recv_r, 2, True))

    @pl.when(conc)
    def _():
        def pool(step):
            n = NS // CH
            away = (step + 1) // 2
            i = lax.rem(z // (Z // n) + n // 2 + n + away * (1 - 2 * lax.rem(step, 2)), n)
            ent = entries(i, CH)
            cnt = dot(ent, tile_c)
            slt = dot(ent, tile_s)
            group = lax.shift_right_logical(iota((CH, W), 1), 3)
            parts = [
                jnp.where(slt == (group + 16 * q).astype(F32), cnt, 0.0).astype(BF) for q in range(NB // 16)
            ]
            wide = jnp.concatenate(parts, axis=1) if len(parts) > 1 else parts[0]
            got = dot(wide, recv_t[...].reshape(NB * 8, W))
            per = CH // (G * 8)
            pooled[pl.ds(i * per, per)] = got.astype(BF).reshape(per, G * 8, W)

            def send(q):
                zz = i * per + q

                @pl.when(zz != z)
                def _():
                    remote(pooled.at[zz], mid_p.at[z // M], 3, dp_of(g, zz), m)

                @pl.when(zz == z)
                def _():
                    local(pooled.at[zz], mid_p.at[z // M], 3)

            each(0, per, send)

        each(0, NS // CH, pool)

    sent_if(conc, lambda: wait_out(pooled.at[pl.ds(0, Z - 1)], 3))
    ins["pooled"] = lambda: wait_in(mid_p, 3)

    take("pooled")
    send_p[...] = dot(swap_ref[0], mid_p[...].reshape(R2, W)).astype(BF).reshape(G, K * 8, W)
    local(send_p.at[g], slots.at[m * G + g], 4)

    for dp, gg, mm in near:
        remote(send_p.at[gg], slots.at[m * G + g], 4, dp, mm)
    sent(slots.at[pl.ds(0, M * G - 1)], 4)
    ins["slots"] = lambda: wait_in(slots, 4)
    take("slots")

    for i in (5, 6, 9, 10, 11):
        loads[i].wait()
    table_s = slots[...].reshape(NS, W)
    feat[0] = dense_ref[...]
    for f in range(3):
        feat[f + 1] = dot(from_slot[f], table_s).astype(BF)
    features = jnp.concatenate([feat[i] for i in range(4)], axis=1)
    pre = dot(features, w_ref[...]) + b_ref[...]
    sig = jax.nn.sigmoid(pre)
    active = pre * sig
    act[...] = active
    slope[...] = sig * (1.0 + pre * (1.0 - sig)) * wo_ref[...]
    part = jnp.sum(active * wo_ref[...], axis=1, keepdims=True)
    eye_b = iota((B, B), 0) == iota((B, B), 1)
    part_row = jnp.sum(jnp.where(eye_b, part, 0.0), axis=0, keepdims=True)
    lbuf[m] = jnp.broadcast_to(part_row, (8, B))
    each(1, M, lambda t: remote(lbuf.at[m], lbuf.at[m], 3, me, lax.rem(m + t, M), True))
    sent(lbuf.at[pl.ds(0, M - 1)], 3, True)
    ins["logits"] = lambda: wait_in(lbuf.at[pl.ds(0, M - 1)], 3, True)
    eye_w = onehot(iota((W, W), 0) == iota((W, W), 1))
    for i in range(4):
        turned = dot(eye_w, feat[i], ((1,), (1,))).astype(BF)
        feat_t[i // 2, pl.ds((i % 2) * W, W), :] = turned
    take("logits")

    total = lbuf[0]
    for i in range(1, M):
        total = total + lbuf[i]
    lgrad_row = jax.nn.sigmoid(total[0:1, :]) - label_ref[...].astype(F32)
    lgrad = to_col(lgrad_row, B, eye_b)
    grad_pre = lgrad * slope[...]
    grad_low = grad_pre.astype(BF)
    hrows = 512 // C
    other = 1 - c
    mate = me + 1 - 2 * c

    for q in range(S.Q):
        send_c[q] = dot(feat_t[other], grad_low[:, q * S.HQ : (q + 1) * S.HQ]).astype(BF)
        remote(send_c.at[q], recv_c.at[q], 16 + q, mate, m)
        sent(send_c.at[q], 16 + q)
        ins["core", q] = lambda q=q: wait_in(recv_c.at[q], 16 + q)
    for q in range(S.Q):
        keep_c[q] = dot(feat_t[c], grad_low[:, q * S.HQ : (q + 1) * S.HQ])

    for f in range(3):
        term = dot(grad_low, w_ref[pl.ds((f + 1) * W, W), :], ((1,), (1,)))
        inputs[pl.ds(f * B, B), :] = term.astype(BF)
    for q in range(S.Q):
        take(("core", q))
        keep_y[q] = keep_c[q] + recv_c[q].astype(F32)
        send_y[q] = keep_y[q].astype(BF).reshape(Y, S.RY, S.HQ)

        def to_y(t):
            yy = lax.rem(y + t, Y)
            remote(send_y.at[q, yy], recv_y.at[q, y], 18 + q, (yy * Z + z) * C + c, m)

        each(1, Y, to_y)
        sent(send_y.at[q, pl.ds(0, Y - 1)], 18 + q)
        ins["dense_y", q] = lambda q=q: wait_in(recv_y.at[q, pl.ds(0, Y - 1)], 18 + q)
    for q in range(M):
        part_s[q] = dot(to_slot[q], inputs[...]).astype(BF).reshape(G, K * 8, W)

    local(part_s.at[m, g], recv_x.at[m * G + g], 7)
    for dp, gg, mm in near:
        remote(part_s.at[mm, gg], recv_x.at[m * G + g], 7, dp, mm)
    sent(recv_x.at[pl.ds(0, M * G - 1)], 7)
    ins["bags_x"] = lambda: wait_in(recv_x, 7)

    b1 = jnp.sum(grad_pre, axis=0, keepdims=True)
    w2 = jnp.sum(lgrad * act[...], axis=0, keepdims=True)
    for i, row in enumerate((b1, w2)):
        for j in range(HL // W):
            vec[i, j // S.V, pl.ds(j % S.V, 1), :] = row[:, j * W : (j + 1) * W]

    remote(vec.at[other], vec_c, 6, mate, m, True)
    sent(vec_c, 6, True)
    ins["core_v"] = lambda: wait_in(vec_c, 6, True)


    take("core_v")
    vec[c] = vec[c] + vec_c[...]

    def to_y_vec(t):
        yy = lax.rem(y + t, Y)
        remote(vec.at[c, yy], vec_y.at[y], 8, (yy * Z + z) * C + c, m, True)

    each(1, Y, to_y_vec)
    sent(vec_y.at[pl.ds(0, Y - 1)], 8, True)
    ins["dense_yv"] = lambda: wait_in(vec_y.at[pl.ds(0, Y - 1)], 8, True)

    def dense_z(q):
        take(("dense_y", q))
        acc = keep_y[q, pl.ds(pl.multiple_of(y * S.RY, S.RY), S.RY), :]
        for t in range(1, Y):
            acc = acc + recv_y[q, lax.rem(y + t, Y)].astype(F32)
        for i in range(Z):
            r0, c0 = (i // S.CG) * S.pr, (i % S.CG) * S.pc
            send_z[q, i] = acc[r0 : r0 + S.pr, c0 : c0 + S.pc].astype(BF)
        local(send_z.at[q, z], recv_z.at[q, z], 20 + q)

        def to_z(zz):
            remote(send_z.at[q, zz], recv_z.at[q, z], 20 + q, dp_of(g, zz), m)

        along_z(to_z)
        sent(send_z.at[q, pl.ds(0, Z - 1)], 20 + q)
        ins["dense_z", q] = lambda: wait_in(recv_z.at[q], 20 + q)

    for q in range(S.Q):
        dense_z(q)

    take("bags_x")
    total = recv_x[pl.ds(0, G)].astype(F32)
    for i in range(1, M):
        total = total + recv_x[pl.ds(i * G, G)].astype(F32)
    send_h[...] = dot(swap_ref[1], total.astype(BF).reshape(R2, W)).astype(BF).reshape(K, G * 8, W)

    def grad_b(k):
        zz = base_z + M * k

        @pl.when(zz != z)
        def _():
            remote(send_h.at[k], recv_g.at[z], 11, dp_of(g, zz), m)

        @pl.when(zz == z)
        def _():
            local(send_h.at[k], recv_g.at[z], 11)

    each(0, K, grad_b)

    def grad_b_sent(n):
        if n:
            wait_out(send_h.at[pl.ds(0, n)], 11)

    sent_if(conc, lambda: grad_b_sent(K - 1))
    sent_if(jnp.logical_not(conc), lambda: grad_b_sent(K))
    ins["grads"] = lambda: pl.when(conc)(lambda: wait_in(recv_g, 11))


    take("dense_yv")
    accv = vec[c, y]
    for t in range(1, Y):
        accv = accv + vec_y[lax.rem(y + t, Y)]
    vec_ys[...] = accv
    local(vec_ys, vec_z.at[z], 10, True)
    along_z(lambda zz: remote(vec_ys, vec_z.at[z], 10, dp_of(g, zz), m, True))
    sent(vec_z.at[pl.ds(0, Z - 1)], 10, True)
    ins["dense_zv"] = lambda: wait_in(vec_z, 10, True)
    def cast_t():
        for h in range(2):
            part = recv_t.at[pl.ds(h * (Z // 2), Z // 2)]
            each(1, M, lambda t: remote(part, part, 2, me, lax.rem(m + t, M)))

    def cast_t_sent():
        for _ in range(M - 1):
            wait_out(recv_t, 2)

    pl.when(conc)(cast_t)
    sent_if(conc, cast_t_sent)
    ins["cast_t"] = lambda: pl.when(jnp.logical_not(conc))(lambda: wait_in(recv_t, 2))


    block0 = c * hrows + y * S.RY

    def gather_z(q):
        take(("dense_z", q))

        def add_z(i, carry):
            return carry + recv_z[q, i].astype(F32)

        acc = lax.fori_loop(0, Z, add_z, jnp.zeros((S.pr, S.pc), F32))
        r0 = pl.multiple_of(block0 + (z // S.CG) * S.pr, 16)
        c0 = pl.multiple_of(q * S.HQ + lax.rem(z, S.CG) * S.pc, W)
        out_w[pl.ds(r0, S.pr), pl.ds(c0, S.pc)] = acc.astype(BF)
        piece = out_w.at[pl.ds(r0, S.pr), pl.ds(c0, S.pc)]
        along_z(lambda zz: remote(piece, piece, 22 + q, dp_of(g, zz), m))
        sent(send_z.at[q, pl.ds(0, Z - 1)], 22 + q)
        ins["out_z", q] = lambda: wait_in(send_z.at[q, pl.ds(0, Z - 1)], 22 + q)


    for q in range(S.Q):
        gather_z(q)
    take("cast_r")
    sel = onehot((iota((16, W), 1) & 15) == iota((16, W), 0))
    lists = dot(sel, entries(0, NS), ((1,), (1,)))
    list8 = lists[0:8, :]
    slot_row = lists[8:9, :]
    take("grads")

    @pl.when(conc)
    def _():
        each(1, M, lambda t: remote(recv_g, recv_g, 13, me, lax.rem(m + t, M)))

    def grads_sent():
        for _ in range(M - 1):
            wait_out(recv_g, 13)

    sent_if(conc, grads_sent)
    ins["grads_x"] = lambda: pl.when(jnp.logical_not(conc))(lambda: wait_in(recv_g, 13))

    take("dense_zv")
    accv = vec_z[0]
    for i in range(1, Z):
        accv = accv + vec_z[i]
    out_v[c, y] = accv

    def ag_yv(t):
        yy = lax.rem(y + t, Y)
        remote(out_v.at[c, y], out_v.at[c, y], 14, (yy * Z + z) * C + c, m, True)

    each(1, Y, ag_yv)
    sent(out_v.at[0, pl.ds(0, Y - 1)], 14, True)
    ins["out_yv"] = lambda: wait_in(out_v.at[0, pl.ds(0, Y - 1)], 14, True)

    QR = G * 16

    def update(pair):
        for i in (2 * pair, 2 * pair + 1):
            update_one(i)

    def update_one(i):
        row = iota((QR, 1), 0)
        slot_id = (lax.shift_right_logical(row, 3) + i * (QR // 8)).astype(F32)
        cnt = jnp.broadcast_to(list8[None], (QR // 8, 8, NS)).reshape(QR, NS)
        wide = jnp.where(slot_row == slot_id, cnt, 0.0).astype(BF)
        grad = dot(wide, recv_g[...].reshape(NS, W))
        src_rows = recv_r[i]
        wide_s = jnp.broadcast_to(src_rows[:, None, :], (G, 16, W)).reshape(QR, W)
        pick_s = iota((QR, W), 1) == (iota((QR, W), 0) & 15) + 96
        st = jnp.sum(jnp.where(pick_s, wide_s, 0.0), axis=1, keepdims=True)
        st = st + jnp.sum(grad * grad, axis=1, keepdims=True) * (1.0 / W)
        low = recv_t[i].reshape(QR, W)
        step = (learn_rate * grad / (jnp.sqrt(st) + epsilon)).astype(BF)
        pick_o = iota((QR, W), 1) == (iota((QR, W), 0) & 7)
        st8 = jnp.sum(jnp.where(pick_o, st, 0.0).reshape(QR // 8, 8, W), axis=1)
        for q in range(Y):
            at = pl.ds(pl.multiple_of((q * Z + i) * 32, 32), 32)
            out_t[at, :] = low[q * 32 : (q + 1) * 32]
            out_d[at, :] = step[q * 32 : (q + 1) * 32]
            stage_s[pl.ds((q * Z + i) * 4, 4), :] = st8[q * 4 : (q + 1) * 4]

    for q in range(S.Q):
        take(("out_z", q))
        mine = out_w.at[pl.ds(pl.multiple_of(block0, 16), S.RY), pl.ds(q * S.HQ, S.HQ)]

        def ag_y(t):
            yy = lax.rem(y + t, Y)
            remote(mine, mine, 24 + q, (yy * Z + z) * C + c, m)

        each(1, Y, ag_y)
        sent(send_y.at[q, pl.ds(0, Y - 1)], 24 + q)
        ins["out_y", q] = lambda q=q: wait_in(send_y.at[q, pl.ds(0, Y - 1)], 24 + q)

    take("cast_t")
    take("grads_x")
    each(0, Z // 2, update)

    writes = []

    def write(src, dst, i):
        writes.append(pltpu.make_async_copy(src, dst, out_sem.at[i]))
        writes[-1].start()

    write(out_t, results[0], 0)
    write(out_d, results[1], 1)

    def gather_core(q):
        take(("out_y", q))
        part = out_w.at[pl.ds(pl.multiple_of(c * hrows, 16), hrows), pl.ds(q * S.HQ, S.HQ)]
        remote(part, part, 26 + q, mate, m)
        sent(send_c.at[q], 26 + q)
        ins["out_c", q] = lambda: wait_in(recv_c.at[q], 26 + q)

    for q in range(S.Q):
        gather_core(q)
    take("out_yv")
    remote(out_v.at[c], out_v.at[c], 15, mate, m, True)
    sent(vec_c, 15, True)
    ins["out_cv"] = lambda: wait_in(vec_c, 15, True)
    own = pl.ds(pl.multiple_of(c * hrows, 16), hrows)
    write(out_w.at[own], results[3].at[own], 3)
    out_s[...] = jnp.transpose(stage_s[...])[0:8, :]
    write(out_s, results[2], 2)
    take("out_cv")
    for q in range(S.Q):
        take(("out_c", q))
    far = pl.ds(pl.multiple_of(other * hrows, 16), hrows)
    write(out_w.at[far], results[3].at[far], 4)
    write(out_v, results[4], 5)
    assert not ins
    for copy in writes:
        copy.wait()

    for done in outs:
        done()


def local_step(
    dense_input,
    labels,
    table,
    adagrad_state,
    new_owner,
    bag_owner,
    bag_slot,
    bag_offsets,
    bag_length,
    w_first,
    b_first,
    w_out,
):
    blocks = table.shape[0]
    samples = dense_input.shape[0]
    hidden = w_first.shape[1]
    S = Shape(lax.axis_size("dp"), lax.axis_size("mp"), blocks, samples, hidden)
    C, Y, Z, M, K, G, N = S.C, S.Y, S.Z, S.M, S.K, S.G, S.N
    R2 = K * G * 8
    V = pltpu.VMEM
    hrows = 512 // C
    args = (
        new_owner.reshape(1, blocks),
        bag_owner.reshape(1, 3 * samples),
        bag_slot,
        bag_offsets.T,
        bag_length,
        dense_input,
        labels.reshape(1, samples),
        table.reshape(blocks * 8, W),
        adagrad_state.T,
        w_first,
        b_first.reshape(1, hidden),
        w_out.reshape(1, hidden),
    )
    made = (
        jax.ShapeDtypeStruct((blocks * 8, W), BF),
        jax.ShapeDtypeStruct((blocks * 8, W), BF),
        jax.ShapeDtypeStruct((8, blocks), F32),
        jax.ShapeDtypeStruct((512, hidden), BF),
        jax.ShapeDtypeStruct((C, Y, S.V, W), F32),
    )
    out_t, out_d, out_s, out_w, out_v = pl.pallas_call(
        functools.partial(kernel, S),
        out_shape=made,
        in_specs=[pl.BlockSpec(memory_space=pltpu.HBM)] * 12,
        out_specs=(pl.BlockSpec(memory_space=pl.ANY),) * 5,
        scratch_shapes=[
            V((blocks, W), F32),
            V((2 * S.T * 8, W), F32),
            V((G, K, 16, W), BF),
            V((G, K, 1, W), F32),
            V((G, K, 16, W), BF),
            V((G, K, 1, W), F32),
            V((K, G, W), F32),
            V((Z, G, 16, W), BF),
            V((Z, G, W), F32),
            V((Z, G * 8, W), BF),
            V((K, G * 8, W), BF),
            V((G, K * 8, W), BF),
            V((M * G, K * 8, W), BF),
            V((M, 8, samples), F32),
            V((samples, hidden), F32),
            V((samples, hidden), F32),
            V((4, samples, W), BF),
            V((C, 2 * W, samples), BF),
            V((3, samples, S.N * 8), BF),
            V((M, R2, 3 * samples), BF),
            V((2, R2, R2), BF),
            V((3 * samples, W), BF),
            V((M, G, K * 8, W), BF),
            V((M * G, K * 8, W), BF),
            V((K, G * 8, W), BF),
            V((Z, G * 8, W), BF),
            V((S.Q, hrows, S.HQ), BF),
            V((S.Q, hrows, S.HQ), F32),
            V((S.Q, hrows, S.HQ), BF),
            V((S.Q, Y, S.RY, S.HQ), BF),
            V((S.Q, hrows, S.HQ), F32),
            V((S.Q, Y, S.RY, S.HQ), BF),
            V((S.Q, Z, S.pr, S.pc), BF),
            V((S.Q, Z, S.pr, S.pc), BF),
            V((C, Y, S.V, W), F32),
            V((Y, S.V, W), F32),
            V((Y, S.V, W), F32),
            V((S.V, W), F32),
            V((Z, S.V, W), F32),
            pltpu.SemaphoreType.DMA((32,)),
            pltpu.SemaphoreType.DMA((32,)),
            pltpu.SemaphoreType.DMA((32,)),
            pltpu.SemaphoreType.DMA((32,)),
            pltpu.SemaphoreType.DMA((12,)),
            pltpu.SemaphoreType.DMA((6,)),
        ]
        + [V(a.shape, a.dtype) for a in args + made],
        compiler_params=pltpu.CompilerParams(
            collective_id=0, has_side_effects=True, vmem_limit_bytes=56 * 1024 * 1024
        ),
    )(*args)
    vecs = out_v.reshape(C, hidden)
    return (
        lax.optimization_barrier(out_t.astype(F32) - out_d.astype(F32)).reshape(blocks, 8, W),
        out_s.T,
        out_w,
        vecs[0],
        vecs[1],
    )


def solution(mesh):
    placed = (
        P("dp", None),
        P("dp"),
        P("dp", None, None),
        P("dp", None),
        P("dp"),
        P("dp", None),
        P("dp"),
        P("dp", None),
        P("dp"),
        P(None, "mp"),
        P("mp"),
        P("mp"),
    )
    return jax.shard_map(
        local_step,
        mesh=mesh,
        in_specs=placed,
        out_specs=(P("dp", None, None), P("dp", None), P(None, "mp"), P("mp"), P("mp")),
        check_vma=False,
    )
```

```python
import functools

import jax
import jax.numpy as jnp
from jax import lax
from jax.experimental import pallas as pl
from jax.experimental.pallas import tpu as pltpu
from jax.sharding import PartitionSpec as P

MESH = pl.DeviceIdType.MESH
BF = jnp.bfloat16
F32 = jnp.float32
I32 = jnp.int32
learn_rate = 0.01
epsilon = 1e-08
W = 128


def iota(shape, dim):
    return lax.broadcasted_iota(I32, shape, dim)


def dot(a, b, dims=((1,), (0,)), exact=False):
    return lax.dot_general(
        a,
        b,
        (dims, ((), ())),
        precision=lax.Precision.HIGHEST if exact else None,
        preferred_element_type=F32,
    )


def log2(n):
    return n.bit_length() - 1


def onehot(mask):
    return jnp.where(mask, 1.0, 0.0).astype(BF)


def to_col(row, rows, pick):
    return jnp.sum(jnp.where(pick, row, 0.0), axis=1, keepdims=True)


class Shape:
    def __init__(self, dp, mp, blocks, samples, hidden):
        self.C = 2
        self.Y = 4 if dp == 128 else 2
        self.Z = dp // (self.C * self.Y)
        self.M = mp
        self.K = self.Z // mp
        self.G = self.Y * self.C
        self.N = dp
        self.NB = blocks
        self.B = samples
        self.HL = hidden
        self.T = self.G * self.K
        self.RY = 512 // (self.C * self.Y)
        self.RG = min(self.Z, self.RY // 16)
        self.CG = self.Z // self.RG
        self.pr = self.RY // self.RG
        self.Q = 2
        self.HQ = hidden // self.Q
        self.pc = self.HQ // self.CG
        self.V = hidden // (W * self.Y)


def kernel(
    S,
    *refs,
):
    given, results, rest = refs[:12], refs[12:16], refs[16:]
    held, made, inner = rest[-16:-4], rest[-4:], rest[:-16]
    run(S, given, held, results, *made, *inner)


def run(
    S,
    given,
    held,
    results,
    out_t,
    out_s,
    out_w,
    out_v,
    stage_s,
    stage_t,
    send_t,
    send_r,
    mid_t,
    mid_r,
    mid_q,
    recv_t,
    recv_r,
    pooled,
    mid_p,
    send_p,
    slots,
    lbuf,
    act,
    slope,
    feat,
    feat_t,
    from_slot,
    to_slot,
    swap_ref,
    inputs,
    part_s,
    recv_x,
    send_h,
    recv_g,
    send_c,
    keep_c,
    recv_c,
    send_y,
    keep_y,
    recv_y,
    send_z,
    recv_z,
    vec,
    vec_c,
    vec_y,
    vec_ys,
    vec_z,
    ss,
    rs,
    sr,
    rr,
    in_sem,
    out_sem,
):
    (owner_ref, bown_ref, bslot_ref, boff_ref, blen_ref, dense_ref, label_ref, table_ref, state_ref, w_ref, b_ref, wo_ref) = held
    C, Y, Z, M, K, G, N, NB, B, HL, T = S.C, S.Y, S.Z, S.M, S.K, S.G, S.N, S.NB, S.B, S.HL, S.T
    B3 = 3 * B
    NS = N * 8
    lY, lZ, lM, lK, lG = log2(Y), log2(Z), log2(M), log2(K), log2(G)
    me = lax.axis_index("dp")
    m = lax.axis_index("mp")
    c = lax.rem(me, C)
    z = lax.rem(me // C, Z)
    y = me // (C * Z)
    g = y * C + c
    half = M // 2
    home = lax.rem(z + half * c, M)
    conc = home == m
    base_z = lax.rem(m + M - half * c, M)

    def dp_of(gg, zz):
        return ((gg // C) * Z + zz) * C + lax.rem(gg, C)

    def remote(src, dst, i, dp, mp, small=False):
        pltpu.make_async_remote_copy(
            src_ref=src,
            dst_ref=dst,
            send_sem=(sr if small else ss).at[i],
            recv_sem=(rr if small else rs).at[i],
            device_id=(dp, mp),
            device_id_type=MESH,
        ).start()

    def local(src, dst, i, small=False):
        pltpu.make_async_copy(src, dst, (rr if small else rs).at[i]).start()

    def wait_in(ref, i, small=False):
        pltpu.make_async_copy(ref, ref, (rr if small else rs).at[i]).wait()

    def wait_out(ref, i, small=False):
        pltpu.make_async_copy(ref, ref, (sr if small else ss).at[i]).wait()

    ins = {}
    outs = []

    def take(name):
        ins.pop(name)()

    def sent(ref, i, small=False):
        outs.append(lambda: wait_out(ref, i, small))

    def sent_if(cond, body):
        outs.append(lambda: pl.when(cond)(body))

    def each(lo, hi, body):
        def step(t, carry):
            body(t)
            return carry

        lax.fori_loop(lo, hi, step, 0)

    barrier = pltpu.get_barrier_semaphore()

    def greet(dp, mp):
        pl.semaphore_signal(barrier, inc=1, device_id=(dp, mp), device_id_type=MESH)

    ys = [lax.rem(y + i, Y) for i in range(Y)]
    cs = [c, 1 - c]
    ms = [lax.rem(m + i, M) for i in range(M)]
    steps = [(i, j, k) for i in range(Y) for j in range(C) for k in range(M) if (i, j, k) != (0, 0, 0)]
    steps.sort(key=lambda a: -(min(a[0], Y - a[0]) + min(a[2], M - a[2])))
    near = [((ys[i] * Z + z) * C + cs[j], ys[i] * C + cs[j], ms[k]) for i, j, k in steps]

    def along_z(body):
        def step(i):
            away = (i + 1) // 2
            body(lax.rem(z + Z // 2 + Z + away * (1 - 2 * lax.rem(i, 2)), Z))

        each(0, Z - 1, step)

    along_z(lambda zz: greet(dp_of(g, zz), m))
    loads = [pltpu.make_async_copy(a, h, in_sem.at[i]) for i, (a, h) in enumerate(zip(given, held))]
    for load in loads:
        load.start()
    for dp, _, mm in near:
        greet(dp, mm)

    for i in (0, 7):
        loads[i].wait()

    def target_of(tt):
        gg = lax.shift_right_logical(tt, lK)
        kk = tt & (K - 1)
        yy = lax.shift_right_logical(gg, 1)
        cc = gg & 1
        zz = ((m + M - half * cc) & (M - 1)) + M * kk
        return (yy * Z + zz) * C + cc

    own_row = owner_ref[...].astype(F32)
    own_col = to_col(own_row, NB, iota((NB, NB), 0) == iota((NB, NB), 1))
    rank_row = jnp.sum(
        jnp.where((own_col == own_row) & (iota((NB, NB), 0) < iota((NB, NB), 1)), 1.0, 0.0),
        axis=0,
        keepdims=True,
    )
    rows2 = iota((2 * T, 1), 0)
    want = target_of(lax.shift_right_logical(rows2, 1)).astype(F32)
    pick_f = jnp.where((own_row == want) & (rank_row == (rows2 & 1).astype(F32)), 1.0, 0.0)
    pick = pick_f.astype(BF)
    for r in range(8):
        low = table_ref[pl.ds(r, NB, stride=8), :].astype(BF)
        stage_t[pl.ds(r, 2 * T, stride=8), :] = dot(pick, low)
    send_t[...] = stage_t[...].astype(BF).reshape(G, K, 16, W)

    pl.semaphore_wait(barrier, (M * G - 1) + (Z - 1))

    local(send_t.at[g], mid_t.at[g], 0)
    group = [(dp, gg) for (dp, gg, _), (_, _, k) in zip(near, steps) if k == 0]
    for dp, gg in group:
        remote(send_t.at[gg], mid_t.at[g], 0, dp, m)
    sent(mid_t.at[pl.ds(0, G - 1)], 0)
    ins["mid_t"] = lambda: wait_in(mid_t, 0)

    for i in (1, 2, 3, 4, 8):
        loads[i].wait()
    bo = bown_ref[...]
    bo_row = bo.astype(F32)
    bo_col = to_col(bo_row, B3, iota((B3, B3), 0) == iota((B3, B3), 1))
    brank_row = jnp.sum(
        jnp.where((bo_col == bo_row) & (iota((B3, B3), 0) < iota((B3, B3), 1)), 1.0, 0.0),
        axis=0,
        keepdims=True,
    )
    slot_nat = bslot_ref[...].reshape(1, B3)
    sy = lax.shift_right_logical(slot_nat, lZ + 2)
    sz = lax.shift_right_logical(slot_nat, 2) & (Z - 1)
    slot_z = ((sz * Y + sy) * 4 + (slot_nat & 3)).astype(F32)
    live = iota((16, B3), 0) < blen_ref[...].reshape(1, B3)
    offs = jnp.where(live, boff_ref[...], -1)
    cnts = [jnp.sum(jnp.where(offs == o, 1.0, 0.0), axis=0, keepdims=True) for o in range(8)]
    line = iota((8, B3), 0)
    cnt8 = jnp.zeros((8, B3), F32)
    for o in range(8):
        cnt8 = jnp.where(line == o, cnts[o], cnt8)
    one16 = jnp.concatenate([cnt8, jnp.where(line == 0, slot_z, 0.0)], axis=0)
    req = jnp.concatenate([one16] * 8, axis=0)
    req = jnp.where(lax.shift_right_logical(iota((W, B3), 0), 4).astype(F32) == brank_row, req, 0.0).astype(BF)
    want_t = target_of(iota((T, 1), 0)).astype(F32)
    rows = dot(onehot(bo_row == want_t), req, ((1,), (1,)))
    for p in range(2):
        pad = [jnp.zeros((96 + 8 * p, NB), F32), state_ref[...], jnp.zeros((24 - 8 * p, NB), F32)]
        pick_p = jnp.where((own_row == want_t) & (rank_row == float(p)), 1.0, 0.0)
        rows = rows + dot(pick_p, jnp.concatenate(pad, axis=0), ((1,), (1,)), exact=True)
    for t in range(T):
        send_r[t // K, t % K] = rows[t : t + 1, :]

    local(send_r.at[g], mid_r.at[g], 0, True)
    for dp, gg in group:
        remote(send_r.at[gg], mid_r.at[g], 0, dp, m, True)
    sent(mid_r.at[pl.ds(0, G - 1)], 0, True)
    ins["mid_r"] = lambda: wait_in(mid_r, 0, True)

    def fwd_b(mid, recv, small):
        def to(k):
            zz = base_z + M * k

            @pl.when(zz != z)
            def _():
                remote(mid(k), recv.at[z], 1, dp_of(g, zz), m, small)

            @pl.when(zz == z)
            def _():
                local(mid(k), recv.at[z], 1, small)

        each(0, K, to)

    take("mid_t")
    fwd_b(lambda k: mid_t.at[:, k], recv_t, False)
    take("mid_r")
    for t in range(T):
        mid_q[t % K, pl.ds(t // K, 1), :] = mid_r[t // K, t % K]
    fwd_b(lambda k: mid_q.at[k], recv_r, True)

    def fwd_b_sent(n):
        if n:
            wait_out(recv_r.at[pl.ds(0, n)], 1, True)
            wait_out(recv_t.at[pl.ds(0, n)], 1)

    sent_if(conc, lambda: fwd_b_sent(K - 1))
    sent_if(jnp.logical_not(conc), lambda: fwd_b_sent(K))

    def wait_blocks():
        wait_in(recv_r, 1, True)
        wait_in(recv_t, 1)

    ins["blocks"] = lambda: pl.when(conc)(wait_blocks)

    oc = bo & 1
    oz = lax.shift_right_logical(bo, 1) & (Z - 1)
    oy = lax.shift_right_logical(bo, 1 + lZ)
    om = (oz + half * oc) & (M - 1)
    ok = lax.shift_right_logical(oz, lM)
    place = (((om * G + oy * C + oc) * K + ok) * 8).astype(F32) + brank_row
    pcol, prow = [], []
    for f in range(3):
        col = to_col(place, B, iota((B, B3), 1) == 3 * iota((B, B3), 0) + f)
        pcol.append(col)
        prow.append(jnp.sum(jnp.where(iota((B, B), 0) == iota((B, B), 1), col, 0.0), axis=0, keepdims=True))

    low16 = iota((W, W), 0) & 15
    tile_c = onehot(low16 == (iota((W, W), 1) & 7))
    tile_s = onehot(low16 == 8)

    CH = min(NS, 2 * G * 8)

    def entries(i, n):
        row = iota((n, N), 0) + i * n
        src = onehot(lax.shift_right_logical(row, 3) == iota((n, N), 1))
        wide = dot(src, jnp.where(iota((N, W), 1) < 96, recv_r[...].reshape(N, W), 0.0).astype(BF))
        keep = lax.shift_right_logical(iota((n, W), 1), 4) == (iota((n, W), 0) & 7)
        return jnp.where(keep, wide, 0.0).astype(BF)

    R2 = K * G * 8
    ro = iota((R2, R2), 0)
    ri = iota((R2, R2), 1)
    for i, (a, b) in enumerate(((ro, ri), (ri, ro))):
        swap_ref[i] = onehot(
            (lax.shift_right_logical(a, lK + 3) == (lax.shift_right_logical(b, 3) & (G - 1)))
            & ((lax.shift_right_logical(a, 3) & (K - 1)) == lax.shift_right_logical(b, lG + 3))
            & ((a & 7) == (b & 7))
        )
    for f in range(3):
        from_slot[f] = onehot(iota((B, NS), 1).astype(F32) == pcol[f])
        for q in range(M):
            to_slot[q, :, f * B : (f + 1) * B] = onehot((iota((R2, B), 0) + q * R2).astype(F32) == prow[f])

    take("blocks")

    def cast_r():
        each(1, M, lambda t: remote(recv_r, recv_r, 2, me, lax.rem(m + t, M), True))

    def cast_r_sent():
        for _ in range(M - 1):
            wait_out(recv_r, 2, True)

    pl.when(conc)(cast_r)
    sent_if(conc, cast_r_sent)
    ins["cast_r"] = lambda: pl.when(jnp.logical_not(conc))(lambda: wait_in(recv_r, 2, True))

    @pl.when(conc)
    def _():
        def pool(step):
            n = NS // CH
            away = (step + 1) // 2
            i = lax.rem(z // (Z // n) + n // 2 + n + away * (1 - 2 * lax.rem(step, 2)), n)
            ent = entries(i, CH)
            cnt = dot(ent, tile_c)
            slt = dot(ent, tile_s)
            group = lax.shift_right_logical(iota((CH, W), 1), 3)
            parts = [
                jnp.where(slt == (group + 16 * q).astype(F32), cnt, 0.0).astype(BF) for q in range(NB // 16)
            ]
            wide = jnp.concatenate(parts, axis=1) if len(parts) > 1 else parts[0]
            got = dot(wide, recv_t[...].reshape(NB * 8, W))
            per = CH // (G * 8)
            pooled[pl.ds(i * per, per)] = got.astype(BF).reshape(per, G * 8, W)

            def send(q):
                zz = i * per + q

                @pl.when(zz != z)
                def _():
                    remote(pooled.at[zz], mid_p.at[z // M], 3, dp_of(g, zz), m)

                @pl.when(zz == z)
                def _():
                    local(pooled.at[zz], mid_p.at[z // M], 3)

            each(0, per, send)

        each(0, NS // CH, pool)

    sent_if(conc, lambda: wait_out(pooled.at[pl.ds(0, Z - 1)], 3))
    ins["pooled"] = lambda: wait_in(mid_p, 3)

    take("pooled")
    send_p[...] = dot(swap_ref[0], mid_p[...].reshape(R2, W)).astype(BF).reshape(G, K * 8, W)
    local(send_p.at[g], slots.at[m * G + g], 4)

    for dp, gg, mm in near:
        remote(send_p.at[gg], slots.at[m * G + g], 4, dp, mm)
    sent(slots.at[pl.ds(0, M * G - 1)], 4)
    ins["slots"] = lambda: wait_in(slots, 4)
    take("slots")

    for i in (5, 6, 9, 10, 11):
        loads[i].wait()
    table_s = slots[...].reshape(NS, W)
    feat[0] = dense_ref[...]
    for f in range(3):
        feat[f + 1] = dot(from_slot[f], table_s).astype(BF)
    features = jnp.concatenate([feat[i] for i in range(4)], axis=1)
    pre = dot(features, w_ref[...]) + b_ref[...]
    sig = jax.nn.sigmoid(pre)
    active = pre * sig
    act[...] = active
    slope[...] = sig * (1.0 + pre * (1.0 - sig)) * wo_ref[...]
    part = jnp.sum(active * wo_ref[...], axis=1, keepdims=True)
    eye_b = iota((B, B), 0) == iota((B, B), 1)
    part_row = jnp.sum(jnp.where(eye_b, part, 0.0), axis=0, keepdims=True)
    lbuf[m] = jnp.broadcast_to(part_row, (8, B))
    each(1, M, lambda t: remote(lbuf.at[m], lbuf.at[m], 3, me, lax.rem(m + t, M), True))
    sent(lbuf.at[pl.ds(0, M - 1)], 3, True)
    ins["logits"] = lambda: wait_in(lbuf.at[pl.ds(0, M - 1)], 3, True)
    eye_w = onehot(iota((W, W), 0) == iota((W, W), 1))
    for i in range(4):
        turned = dot(eye_w, feat[i], ((1,), (1,))).astype(BF)
        feat_t[i // 2, pl.ds((i % 2) * W, W), :] = turned
    take("logits")

    total = lbuf[0]
    for i in range(1, M):
        total = total + lbuf[i]
    lgrad_row = jax.nn.sigmoid(total[0:1, :]) - label_ref[...].astype(F32)
    lgrad = to_col(lgrad_row, B, eye_b)
    grad_pre = lgrad * slope[...]
    grad_low = grad_pre.astype(BF)
    hrows = 512 // C
    other = 1 - c
    mate = me + 1 - 2 * c

    for q in range(S.Q):
        send_c[q] = dot(feat_t[other], grad_low[:, q * S.HQ : (q + 1) * S.HQ]).astype(BF)
        remote(send_c.at[q], recv_c.at[q], 16 + q, mate, m)
        sent(send_c.at[q], 16 + q)
        ins["core", q] = lambda q=q: wait_in(recv_c.at[q], 16 + q)
    for q in range(S.Q):
        keep_c[q] = dot(feat_t[c], grad_low[:, q * S.HQ : (q + 1) * S.HQ])

    for f in range(3):
        term = dot(grad_low, w_ref[pl.ds((f + 1) * W, W), :], ((1,), (1,)))
        inputs[pl.ds(f * B, B), :] = term.astype(BF)
    for q in range(S.Q):
        take(("core", q))
        keep_y[q] = keep_c[q] + recv_c[q].astype(F32)
        send_y[q] = keep_y[q].astype(BF).reshape(Y, S.RY, S.HQ)

        def to_y(t):
            yy = lax.rem(y + t, Y)
            remote(send_y.at[q, yy], recv_y.at[q, y], 18 + q, (yy * Z + z) * C + c, m)

        each(1, Y, to_y)
        sent(send_y.at[q, pl.ds(0, Y - 1)], 18 + q)
        ins["dense_y", q] = lambda q=q: wait_in(recv_y.at[q, pl.ds(0, Y - 1)], 18 + q)
    for q in range(M):
        part_s[q] = dot(to_slot[q], inputs[...]).astype(BF).reshape(G, K * 8, W)

    local(part_s.at[m, g], recv_x.at[m * G + g], 7)
    for dp, gg, mm in near:
        remote(part_s.at[mm, gg], recv_x.at[m * G + g], 7, dp, mm)
    sent(recv_x.at[pl.ds(0, M * G - 1)], 7)
    ins["bags_x"] = lambda: wait_in(recv_x, 7)

    b1 = jnp.sum(grad_pre, axis=0, keepdims=True)
    w2 = jnp.sum(lgrad * act[...], axis=0, keepdims=True)
    for i, row in enumerate((b1, w2)):
        for j in range(HL // W):
            vec[i, j // S.V, pl.ds(j % S.V, 1), :] = row[:, j * W : (j + 1) * W]

    remote(vec.at[other], vec_c, 6, mate, m, True)
    sent(vec_c, 6, True)
    ins["core_v"] = lambda: wait_in(vec_c, 6, True)


    take("core_v")
    vec[c] = vec[c] + vec_c[...]

    def to_y_vec(t):
        yy = lax.rem(y + t, Y)
        remote(vec.at[c, yy], vec_y.at[y], 8, (yy * Z + z) * C + c, m, True)

    each(1, Y, to_y_vec)
    sent(vec_y.at[pl.ds(0, Y - 1)], 8, True)
    ins["dense_yv"] = lambda: wait_in(vec_y.at[pl.ds(0, Y - 1)], 8, True)

    def dense_z(q):
        take(("dense_y", q))
        acc = keep_y[q, pl.ds(pl.multiple_of(y * S.RY, S.RY), S.RY), :]
        for t in range(1, Y):
            acc = acc + recv_y[q, lax.rem(y + t, Y)].astype(F32)
        for i in range(Z):
            r0, c0 = (i // S.CG) * S.pr, (i % S.CG) * S.pc
            send_z[q, i] = acc[r0 : r0 + S.pr, c0 : c0 + S.pc].astype(BF)
        local(send_z.at[q, z], recv_z.at[q, z], 20 + q)

        def to_z(zz):
            remote(send_z.at[q, zz], recv_z.at[q, z], 20 + q, dp_of(g, zz), m)

        along_z(to_z)
        sent(send_z.at[q, pl.ds(0, Z - 1)], 20 + q)
        ins["dense_z", q] = lambda: wait_in(recv_z.at[q], 20 + q)

    for q in range(S.Q):
        dense_z(q)

    take("bags_x")
    total = recv_x[pl.ds(0, G)].astype(F32)
    for i in range(1, M):
        total = total + recv_x[pl.ds(i * G, G)].astype(F32)
    send_h[...] = dot(swap_ref[1], total.astype(BF).reshape(R2, W)).astype(BF).reshape(K, G * 8, W)

    def grad_b(k):
        zz = base_z + M * k

        @pl.when(zz != z)
        def _():
            remote(send_h.at[k], recv_g.at[z], 11, dp_of(g, zz), m)

        @pl.when(zz == z)
        def _():
            local(send_h.at[k], recv_g.at[z], 11)

    each(0, K, grad_b)

    def grad_b_sent(n):
        if n:
            wait_out(send_h.at[pl.ds(0, n)], 11)

    sent_if(conc, lambda: grad_b_sent(K - 1))
    sent_if(jnp.logical_not(conc), lambda: grad_b_sent(K))
    ins["grads"] = lambda: pl.when(conc)(lambda: wait_in(recv_g, 11))


    take("dense_yv")
    accv = vec[c, y]
    for t in range(1, Y):
        accv = accv + vec_y[lax.rem(y + t, Y)]
    vec_ys[...] = accv
    local(vec_ys, vec_z.at[z], 10, True)
    along_z(lambda zz: remote(vec_ys, vec_z.at[z], 10, dp_of(g, zz), m, True))
    sent(vec_z.at[pl.ds(0, Z - 1)], 10, True)
    ins["dense_zv"] = lambda: wait_in(vec_z, 10, True)
    def cast_t():
        for h in range(2):
            part = recv_t.at[pl.ds(h * (Z // 2), Z // 2)]
            each(1, M, lambda t: remote(part, part, 2, me, lax.rem(m + t, M)))

    def cast_t_sent():
        for _ in range(M - 1):
            wait_out(recv_t, 2)

    pl.when(conc)(cast_t)
    sent_if(conc, cast_t_sent)
    ins["cast_t"] = lambda: pl.when(jnp.logical_not(conc))(lambda: wait_in(recv_t, 2))


    block0 = c * hrows + y * S.RY

    def gather_z(q):
        take(("dense_z", q))

        def add_z(i, carry):
            return carry + recv_z[q, i].astype(F32)

        acc = lax.fori_loop(0, Z, add_z, jnp.zeros((S.pr, S.pc), F32))
        r0 = pl.multiple_of(block0 + (z // S.CG) * S.pr, 16)
        c0 = pl.multiple_of(q * S.HQ + lax.rem(z, S.CG) * S.pc, W)
        out_w[pl.ds(r0, S.pr), pl.ds(c0, S.pc)] = acc.astype(BF)
        piece = out_w.at[pl.ds(r0, S.pr), pl.ds(c0, S.pc)]
        along_z(lambda zz: remote(piece, piece, 22 + q, dp_of(g, zz), m))
        sent(send_z.at[q, pl.ds(0, Z - 1)], 22 + q)
        ins["out_z", q] = lambda: wait_in(send_z.at[q, pl.ds(0, Z - 1)], 22 + q)


    for q in range(S.Q):
        gather_z(q)
    take("cast_r")
    sel = onehot((iota((16, W), 1) & 15) == iota((16, W), 0))
    lists = dot(sel, entries(0, NS), ((1,), (1,)))
    list8 = lists[0:8, :]
    slot_row = lists[8:9, :]
    take("grads")

    @pl.when(conc)
    def _():
        each(1, M, lambda t: remote(recv_g, recv_g, 13, me, lax.rem(m + t, M)))

    def grads_sent():
        for _ in range(M - 1):
            wait_out(recv_g, 13)

    sent_if(conc, grads_sent)
    ins["grads_x"] = lambda: pl.when(jnp.logical_not(conc))(lambda: wait_in(recv_g, 13))

    take("dense_zv")
    accv = vec_z[0]
    for i in range(1, Z):
        accv = accv + vec_z[i]
    out_v[c, y] = accv

    def ag_yv(t):
        yy = lax.rem(y + t, Y)
        remote(out_v.at[c, y], out_v.at[c, y], 14, (yy * Z + z) * C + c, m, True)

    each(1, Y, ag_yv)
    sent(out_v.at[0, pl.ds(0, Y - 1)], 14, True)
    ins["out_yv"] = lambda: wait_in(out_v.at[0, pl.ds(0, Y - 1)], 14, True)

    QR = G * 16

    def update(pair):
        for i in (2 * pair, 2 * pair + 1):
            update_one(i)

    def update_one(i):
        row = iota((QR, 1), 0)
        slot_id = (lax.shift_right_logical(row, 3) + i * (QR // 8)).astype(F32)
        cnt = jnp.broadcast_to(list8[None], (QR // 8, 8, NS)).reshape(QR, NS)
        wide = jnp.where(slot_row == slot_id, cnt, 0.0).astype(BF)
        grad = dot(wide, recv_g[...].reshape(NS, W))
        src_rows = recv_r[i]
        wide_s = jnp.broadcast_to(src_rows[:, None, :], (G, 16, W)).reshape(QR, W)
        pick_s = iota((QR, W), 1) == (iota((QR, W), 0) & 15) + 96
        st = jnp.sum(jnp.where(pick_s, wide_s, 0.0), axis=1, keepdims=True)
        st = st + jnp.sum(grad * grad, axis=1, keepdims=True) * (1.0 / W)
        low = recv_t[i].reshape(QR, W).astype(F32)
        new = low - learn_rate * grad / (jnp.sqrt(st) + epsilon)
        pick_o = iota((QR, W), 1) == (iota((QR, W), 0) & 7)
        st8 = jnp.sum(jnp.where(pick_o, st, 0.0).reshape(QR // 8, 8, W), axis=1)
        for q in range(Y):
            at = pl.ds(pl.multiple_of((q * Z + i) * 32, 32), 32)
            out_t[at, :] = new[q * 32 : (q + 1) * 32]
            stage_s[pl.ds((q * Z + i) * 4, 4), :] = st8[q * 4 : (q + 1) * 4]

    for q in range(S.Q):
        take(("out_z", q))
        mine = out_w.at[pl.ds(pl.multiple_of(block0, 16), S.RY), pl.ds(q * S.HQ, S.HQ)]

        def ag_y(t):
            yy = lax.rem(y + t, Y)
            remote(mine, mine, 24 + q, (yy * Z + z) * C + c, m)

        each(1, Y, ag_y)
        sent(send_y.at[q, pl.ds(0, Y - 1)], 24 + q)
        ins["out_y", q] = lambda q=q: wait_in(send_y.at[q, pl.ds(0, Y - 1)], 24 + q)

    take("cast_t")
    take("grads_x")
    each(0, Z // 2, update)

    writes = []

    def write(src, dst, i):
        writes.append(pltpu.make_async_copy(src, dst, out_sem.at[i]))
        writes[-1].start()

    write(out_t, results[0], 0)

    def gather_core(q):
        take(("out_y", q))
        part = out_w.at[pl.ds(pl.multiple_of(c * hrows, 16), hrows), pl.ds(q * S.HQ, S.HQ)]
        remote(part, part, 26 + q, mate, m)
        sent(send_c.at[q], 26 + q)
        ins["out_c", q] = lambda: wait_in(recv_c.at[q], 26 + q)

    for q in range(S.Q):
        gather_core(q)
    take("out_yv")
    remote(out_v.at[c], out_v.at[c], 15, mate, m, True)
    sent(vec_c, 15, True)
    ins["out_cv"] = lambda: wait_in(vec_c, 15, True)
    own = pl.ds(pl.multiple_of(c * hrows, 16), hrows)
    write(out_w.at[own], results[2].at[own], 3)
    out_s[...] = jnp.transpose(stage_s[...])[0:8, :]
    write(out_s, results[1], 2)
    take("out_cv")
    for q in range(S.Q):
        take(("out_c", q))
    far = pl.ds(pl.multiple_of(other * hrows, 16), hrows)
    write(out_w.at[far], results[2].at[far], 4)
    write(out_v, results[3], 5)
    assert not ins
    for copy in writes:
        copy.wait()

    for done in outs:
        done()


def local_step(
    dense_input,
    labels,
    table,
    adagrad_state,
    new_owner,
    bag_owner,
    bag_slot,
    bag_offsets,
    bag_length,
    w_first,
    b_first,
    w_out,
):
    blocks = table.shape[0]
    samples = dense_input.shape[0]
    hidden = w_first.shape[1]
    S = Shape(lax.axis_size("dp"), lax.axis_size("mp"), blocks, samples, hidden)
    C, Y, Z, M, K, G, N = S.C, S.Y, S.Z, S.M, S.K, S.G, S.N
    R2 = K * G * 8
    V = pltpu.VMEM
    hrows = 512 // C
    args = (
        new_owner.reshape(1, blocks),
        bag_owner.reshape(1, 3 * samples),
        bag_slot,
        bag_offsets.T,
        bag_length,
        dense_input,
        labels.reshape(1, samples),
        table.reshape(blocks * 8, W),
        adagrad_state.T,
        w_first,
        b_first.reshape(1, hidden),
        w_out.reshape(1, hidden),
    )
    made = (
        jax.ShapeDtypeStruct((blocks * 8, W), F32),
        jax.ShapeDtypeStruct((8, blocks), F32),
        jax.ShapeDtypeStruct((512, hidden), BF),
        jax.ShapeDtypeStruct((C, Y, S.V, W), F32),
    )
    found = pl.pallas_call(
        functools.partial(kernel, S),
        out_shape=made,
        in_specs=[pl.BlockSpec(memory_space=pltpu.HBM)] * 12,
        out_specs=(pl.BlockSpec(memory_space=pl.ANY),) * 4,
        scratch_shapes=[
            V((blocks, W), F32),
            V((2 * S.T * 8, W), F32),
            V((G, K, 16, W), BF),
            V((G, K, 1, W), F32),
            V((G, K, 16, W), BF),
            V((G, K, 1, W), F32),
            V((K, G, W), F32),
            V((Z, G, 16, W), BF),
            V((Z, G, W), F32),
            V((Z, G * 8, W), BF),
            V((K, G * 8, W), BF),
            V((G, K * 8, W), BF),
            V((M * G, K * 8, W), BF),
            V((M, 8, samples), F32),
            V((samples, hidden), F32),
            V((samples, hidden), F32),
            V((4, samples, W), BF),
            V((C, 2 * W, samples), BF),
            V((3, samples, S.N * 8), BF),
            V((M, R2, 3 * samples), BF),
            V((2, R2, R2), BF),
            V((3 * samples, W), BF),
            V((M, G, K * 8, W), BF),
            V((M * G, K * 8, W), BF),
            V((K, G * 8, W), BF),
            V((Z, G * 8, W), BF),
            V((S.Q, hrows, S.HQ), BF),
            V((S.Q, hrows, S.HQ), F32),
            V((S.Q, hrows, S.HQ), BF),
            V((S.Q, Y, S.RY, S.HQ), BF),
            V((S.Q, hrows, S.HQ), F32),
            V((S.Q, Y, S.RY, S.HQ), BF),
            V((S.Q, Z, S.pr, S.pc), BF),
            V((S.Q, Z, S.pr, S.pc), BF),
            V((C, Y, S.V, W), F32),
            V((Y, S.V, W), F32),
            V((Y, S.V, W), F32),
            V((S.V, W), F32),
            V((Z, S.V, W), F32),
            pltpu.SemaphoreType.DMA((32,)),
            pltpu.SemaphoreType.DMA((32,)),
            pltpu.SemaphoreType.DMA((32,)),
            pltpu.SemaphoreType.DMA((32,)),
            pltpu.SemaphoreType.DMA((12,)),
            pltpu.SemaphoreType.DMA((6,)),
        ]
        + [V(a.shape, a.dtype) for a in args + made],
        compiler_params=pltpu.CompilerParams(
            collective_id=0, has_side_effects=True, vmem_limit_bytes=56 * 1024 * 1024
        ),
    )(*args)
    part = jax.ShapeDtypeStruct((Y, S.V, W), F32)
    out_t, out_s, out_w, b1, w2 = pl.pallas_call(
        hand_over,
        out_shape=(*made[:3], part, part),
        in_specs=[pl.BlockSpec(memory_space=pl.ANY)] * 4,
        out_specs=(pl.BlockSpec(memory_space=pl.ANY),) * 5,
        scratch_shapes=[V(a.shape, a.dtype) for a in made]
        + [pltpu.SemaphoreType.DMA((11,)), pltpu.SemaphoreType.DMA((11,))],
    )(*found)
    return (
        out_t.reshape(blocks, 8, W),
        out_s.T,
        out_w,
        b1.reshape(hidden),
        w2.reshape(hidden),
    )


def hand_over(t, s, w, v, out_t, out_s, out_w, out_b, out_u, vm_t, vm_s, vm_w, vm_v, sem_in, sem_out):
    trips = []
    for a, x, b in ((t, vm_t, out_t), (w, vm_w, out_w)):
        n = a.shape[0] // 4
        cuts = [pl.ds(i * n, n) for i in range(4)]
        trips += [(a.at[p], x.at[p], b.at[p]) for p in cuts]
    trips += [(s, vm_s, out_s), (v.at[0], vm_v.at[0], out_b), (v.at[1], vm_v.at[1], out_u)]
    come = [pltpu.make_async_copy(a, x, sem_in.at[i]) for i, (a, x, _) in enumerate(trips)]
    go = [pltpu.make_async_copy(x, b, sem_out.at[i]) for i, (_, x, b) in enumerate(trips)]
    for copy in come:
        copy.start()
    for first, then in zip(come, go):
        first.wait()
        then.start()
    for copy in go:
        copy.wait()


def solution(mesh):
    placed = (
        P("dp", None),
        P("dp"),
        P("dp", None, None),
        P("dp", None),
        P("dp"),
        P("dp", None),
        P("dp"),
        P("dp", None),
        P("dp"),
        P(None, "mp"),
        P("mp"),
        P("mp"),
    )
    return jax.shard_map(
        local_step,
        mesh=mesh,
        in_specs=placed,
        out_specs=(P("dp", None, None), P("dp", None), P(None, "mp"), P("mp"), P("mp")),
        check_vma=False,
    )
```

```python
import functools

import jax
import jax.numpy as jnp
from jax import lax
from jax.experimental import pallas as pl
from jax.experimental.pallas import tpu as pltpu
from jax.sharding import PartitionSpec as P

MESH = pl.DeviceIdType.MESH
BF = jnp.bfloat16
F32 = jnp.float32
I32 = jnp.int32
learn_rate = 0.01
epsilon = 1e-08
W = 128


def iota(shape, dim):
    return lax.broadcasted_iota(I32, shape, dim)


def dot(a, b, dims=((1,), (0,)), exact=False):
    return lax.dot_general(
        a,
        b,
        (dims, ((), ())),
        precision=lax.Precision.HIGHEST if exact else None,
        preferred_element_type=F32,
    )


def log2(n):
    return n.bit_length() - 1


def onehot(mask):
    return jnp.where(mask, 1.0, 0.0).astype(BF)


def to_col(row, rows, pick):
    return jnp.sum(jnp.where(pick, row, 0.0), axis=1, keepdims=True)


class Shape:
    def __init__(self, dp, mp, blocks, samples, hidden):
        self.C = 2
        self.Y = 4 if dp == 128 else 2
        self.Z = dp // (self.C * self.Y)
        self.M = mp
        self.K = self.Z // mp
        self.G = self.Y * self.C
        self.N = dp
        self.NB = blocks
        self.B = samples
        self.HL = hidden
        self.T = self.G * self.K
        self.RY = 512 // (self.C * self.Y)
        self.RG = min(self.Z, self.RY // 16)
        self.CG = self.Z // self.RG
        self.pr = self.RY // self.RG
        self.Q = 2
        self.HQ = hidden // self.Q
        self.pc = self.HQ // self.CG
        self.V = hidden // (W * self.Y)


def kernel(
    S,
    *refs,
):
    given, results, rest = refs[:12], refs[12:16], refs[16:]
    held, made, inner = rest[-16:-4], rest[-4:], rest[:-16]
    run(S, given, held, results, *made, *inner)


def run(
    S,
    given,
    held,
    results,
    out_t,
    out_s,
    out_w,
    out_v,
    stage_s,
    stage_t,
    send_t,
    send_r,
    mid_t,
    mid_r,
    mid_q,
    recv_t,
    recv_r,
    pooled,
    mid_p,
    send_p,
    slots,
    lbuf,
    act,
    slope,
    feat,
    feat_t,
    from_slot,
    to_slot,
    swap_ref,
    inputs,
    part_s,
    recv_x,
    send_h,
    recv_g,
    send_c,
    keep_c,
    recv_c,
    send_y,
    keep_y,
    recv_y,
    send_z,
    recv_z,
    vec,
    vec_c,
    vec_y,
    vec_ys,
    vec_z,
    ss,
    rs,
    sr,
    rr,
    in_sem,
    out_sem,
):
    (owner_ref, bown_ref, bslot_ref, boff_ref, blen_ref, dense_ref, label_ref, table_ref, state_ref, w_ref, b_ref, wo_ref) = held
    C, Y, Z, M, K, G, N, NB, B, HL, T = S.C, S.Y, S.Z, S.M, S.K, S.G, S.N, S.NB, S.B, S.HL, S.T
    B3 = 3 * B
    NS = N * 8
    lY, lZ, lM, lK, lG = log2(Y), log2(Z), log2(M), log2(K), log2(G)
    me = lax.axis_index("dp")
    m = lax.axis_index("mp")
    c = lax.rem(me, C)
    z = lax.rem(me // C, Z)
    y = me // (C * Z)
    g = y * C + c
    half = M // 2
    home = lax.rem(z + half * c, M)
    conc = home == m
    base_z = lax.rem(m + M - half * c, M)

    def dp_of(gg, zz):
        return ((gg // C) * Z + zz) * C + lax.rem(gg, C)

    def remote(src, dst, i, dp, mp, small=False):
        pltpu.make_async_remote_copy(
            src_ref=src,
            dst_ref=dst,
            send_sem=(sr if small else ss).at[i],
            recv_sem=(rr if small else rs).at[i],
            device_id=(dp, mp),
            device_id_type=MESH,
        ).start()

    def local(src, dst, i, small=False):
        pltpu.make_async_copy(src, dst, (rr if small else rs).at[i]).start()

    def wait_in(ref, i, small=False):
        pltpu.make_async_copy(ref, ref, (rr if small else rs).at[i]).wait()

    def wait_out(ref, i, small=False):
        pltpu.make_async_copy(ref, ref, (sr if small else ss).at[i]).wait()

    ins = {}
    outs = []

    def take(name):
        ins.pop(name)()

    def sent(ref, i, small=False):
        outs.append(lambda: wait_out(ref, i, small))

    def sent_if(cond, body):
        outs.append(lambda: pl.when(cond)(body))

    def each(lo, hi, body):
        def step(t, carry):
            body(t)
            return carry

        lax.fori_loop(lo, hi, step, 0)

    barrier = pltpu.get_barrier_semaphore()

    def greet(dp, mp):
        pl.semaphore_signal(barrier, inc=1, device_id=(dp, mp), device_id_type=MESH)

    ys = [lax.rem(y + i, Y) for i in range(Y)]
    cs = [c, 1 - c]
    ms = [lax.rem(m + i, M) for i in range(M)]
    steps = [(i, j, k) for i in range(Y) for j in range(C) for k in range(M) if (i, j, k) != (0, 0, 0)]
    steps.sort(key=lambda a: -(min(a[0], Y - a[0]) + min(a[2], M - a[2])))
    near = [((ys[i] * Z + z) * C + cs[j], ys[i] * C + cs[j], ms[k]) for i, j, k in steps]

    def along_z(body):
        def step(i):
            away = (i + 1) // 2
            body(lax.rem(z + Z // 2 + Z + away * (1 - 2 * lax.rem(i, 2)), Z))

        each(0, Z - 1, step)

    along_z(lambda zz: greet(dp_of(g, zz), m))
    loads = [pltpu.make_async_copy(a, h if i != 7 else h.at[pl.ds(0, NB * 8)], in_sem.at[i]) for i, (a, h) in enumerate(zip(given, held))]
    for load in loads:
        load.start()
    for dp, _, mm in near:
        greet(dp, mm)

    loads[0].wait()

    def target_of(tt):
        gg = lax.shift_right_logical(tt, lK)
        kk = tt & (K - 1)
        yy = lax.shift_right_logical(gg, 1)
        cc = gg & 1
        zz = ((m + M - half * cc) & (M - 1)) + M * kk
        return (yy * Z + zz) * C + cc

    own_row = owner_ref[...].astype(F32)
    own_col = to_col(own_row, NB, iota((NB, NB), 0) == iota((NB, NB), 1))
    rank_row = jnp.sum(
        jnp.where((own_col == own_row) & (iota((NB, NB), 0) < iota((NB, NB), 1)), 1.0, 0.0),
        axis=0,
        keepdims=True,
    )
    rows2 = iota((2 * T, 1), 0)
    want = target_of(lax.shift_right_logical(rows2, 1)).astype(F32)
    pick_f = jnp.where((own_row == want) & (rank_row == (rows2 & 1).astype(F32)), 1.0, 0.0)
    pick = pick_f.astype(BF)
    loads[7].wait()
    for r in range(8):
        low = table_ref[pl.ds(r, NB, stride=8), :].astype(BF)
        stage_t[pl.ds(r, 2 * T, stride=8), :] = dot(pick, low)
    send_t[...] = stage_t[pl.ds(0, 2 * T * 8), :].astype(BF).reshape(G, K, 16, W)

    pl.semaphore_wait(barrier, (M * G - 1) + (Z - 1))

    local(send_t.at[g], mid_t.at[g], 0)
    group = [(dp, gg) for (dp, gg, _), (_, _, k) in zip(near, steps) if k == 0]
    for dp, gg in group:
        remote(send_t.at[gg], mid_t.at[g], 0, dp, m)
    sent(mid_t.at[pl.ds(0, G - 1)], 0)
    ins["mid_t"] = lambda: wait_in(mid_t, 0)

    for i in (1, 2, 3, 4, 8):
        loads[i].wait()
    bo = bown_ref[...]
    bo_row = bo.astype(F32)
    bo_col = to_col(bo_row, B3, iota((B3, B3), 0) == iota((B3, B3), 1))
    brank_row = jnp.sum(
        jnp.where((bo_col == bo_row) & (iota((B3, B3), 0) < iota((B3, B3), 1)), 1.0, 0.0),
        axis=0,
        keepdims=True,
    )
    slot_nat = bslot_ref[...].reshape(1, B3)
    sy = lax.shift_right_logical(slot_nat, lZ + 2)
    sz = lax.shift_right_logical(slot_nat, 2) & (Z - 1)
    slot_z = ((sz * Y + sy) * 4 + (slot_nat & 3)).astype(F32)
    live = iota((16, B3), 0) < blen_ref[...].reshape(1, B3)
    offs = jnp.where(live, boff_ref[...], -1)
    cnts = [jnp.sum(jnp.where(offs == o, 1.0, 0.0), axis=0, keepdims=True) for o in range(8)]
    line = iota((8, B3), 0)
    cnt8 = jnp.zeros((8, B3), F32)
    for o in range(8):
        cnt8 = jnp.where(line == o, cnts[o], cnt8)
    one16 = jnp.concatenate([cnt8, jnp.where(line == 0, slot_z, 0.0)], axis=0)
    req = jnp.concatenate([one16] * 8, axis=0)
    req = jnp.where(lax.shift_right_logical(iota((W, B3), 0), 4).astype(F32) == brank_row, req, 0.0).astype(BF)
    want_t = target_of(iota((T, 1), 0)).astype(F32)
    rows = dot(onehot(bo_row == want_t), req, ((1,), (1,)))
    for p in range(2):
        pad = [jnp.zeros((96 + 8 * p, NB), F32), state_ref[...], jnp.zeros((24 - 8 * p, NB), F32)]
        pick_p = jnp.where((own_row == want_t) & (rank_row == float(p)), 1.0, 0.0)
        rows = rows + dot(pick_p, jnp.concatenate(pad, axis=0), ((1,), (1,)), exact=True)
    for t in range(T):
        send_r[t // K, t % K] = rows[t : t + 1, :]

    local(send_r.at[g], mid_r.at[g], 0, True)
    for dp, gg in group:
        remote(send_r.at[gg], mid_r.at[g], 0, dp, m, True)
    sent(mid_r.at[pl.ds(0, G - 1)], 0, True)
    ins["mid_r"] = lambda: wait_in(mid_r.at[pl.ds(0, G)], 0, True)

    def fwd_b(mid, recv, small):
        def to(k):
            zz = base_z + M * k

            @pl.when(zz != z)
            def _():
                remote(mid(k), recv.at[z], 1, dp_of(g, zz), m, small)

            @pl.when(zz == z)
            def _():
                local(mid(k), recv.at[z], 1, small)

        each(0, K, to)

    take("mid_t")
    fwd_b(lambda k: mid_t.at[:, k], recv_t, False)
    take("mid_r")
    for t in range(T):
        mid_q[t % K, pl.ds(t // K, 1), :] = mid_r[t // K, t % K]
    fwd_b(lambda k: mid_q.at[k], recv_r, True)

    def fwd_b_sent(n):
        if n:
            wait_out(recv_r.at[pl.ds(0, n)], 1, True)
            wait_out(recv_t.at[pl.ds(0, n)], 1)

    sent_if(conc, lambda: fwd_b_sent(K - 1))
    sent_if(jnp.logical_not(conc), lambda: fwd_b_sent(K))

    def wait_blocks():
        wait_in(recv_r, 1, True)
        wait_in(recv_t, 1)

    ins["blocks"] = lambda: pl.when(conc)(wait_blocks)

    oc = bo & 1
    oz = lax.shift_right_logical(bo, 1) & (Z - 1)
    oy = lax.shift_right_logical(bo, 1 + lZ)
    om = (oz + half * oc) & (M - 1)
    ok = lax.shift_right_logical(oz, lM)
    place = (((om * G + oy * C + oc) * K + ok) * 8).astype(F32) + brank_row
    pcol, prow = [], []
    for f in range(3):
        col = to_col(place, B, iota((B, B3), 1) == 3 * iota((B, B3), 0) + f)
        pcol.append(col)
        prow.append(jnp.sum(jnp.where(iota((B, B), 0) == iota((B, B), 1), col, 0.0), axis=0, keepdims=True))

    low16 = iota((W, W), 0) & 15
    tile_c = onehot(low16 == (iota((W, W), 1) & 7))
    tile_s = onehot(low16 == 8)

    CH = min(NS, 2 * G * 8)

    def entries(i, n):
        row = iota((n, N), 0) + i * n
        src = onehot(lax.shift_right_logical(row, 3) == iota((n, N), 1))
        wide = dot(src, jnp.where(iota((N, W), 1) < 96, recv_r[...].reshape(N, W), 0.0).astype(BF))
        keep = lax.shift_right_logical(iota((n, W), 1), 4) == (iota((n, W), 0) & 7)
        return jnp.where(keep, wide, 0.0).astype(BF)

    R2 = K * G * 8
    ro = iota((R2, R2), 0)
    ri = iota((R2, R2), 1)
    for i, (a, b) in enumerate(((ro, ri), (ri, ro))):
        swap_ref[i] = onehot(
            (lax.shift_right_logical(a, lK + 3) == (lax.shift_right_logical(b, 3) & (G - 1)))
            & ((lax.shift_right_logical(a, 3) & (K - 1)) == lax.shift_right_logical(b, lG + 3))
            & ((a & 7) == (b & 7))
        )
    for f in range(3):
        from_slot[f] = onehot(iota((B, NS), 1).astype(F32) == pcol[f])
        for q in range(M):
            to_slot[q, :, f * B : (f + 1) * B] = onehot((iota((R2, B), 0) + q * R2).astype(F32) == prow[f])

    take("blocks")

    def cast_r():
        each(1, M, lambda t: remote(recv_r, recv_r, 2, me, lax.rem(m + t, M), True))

    def cast_r_sent():
        for _ in range(M - 1):
            wait_out(recv_r, 2, True)

    pl.when(conc)(cast_r)
    sent_if(conc, cast_r_sent)
    ins["cast_r"] = lambda: pl.when(jnp.logical_not(conc))(lambda: wait_in(recv_r, 2, True))

    @pl.when(conc)
    def _():
        def pool(step):
            n = NS // CH
            away = (step + 1) // 2
            i = lax.rem(z // (Z // n) + n // 2 + n + away * (1 - 2 * lax.rem(step, 2)), n)
            ent = entries(i, CH)
            cnt = dot(ent, tile_c)
            slt = dot(ent, tile_s)
            group = lax.shift_right_logical(iota((CH, W), 1), 3)
            parts = [
                jnp.where(slt == (group + 16 * q).astype(F32), cnt, 0.0).astype(BF) for q in range(NB // 16)
            ]
            wide = jnp.concatenate(parts, axis=1) if len(parts) > 1 else parts[0]
            got = dot(wide, recv_t[...].reshape(NB * 8, W))
            per = CH // (G * 8)
            pooled[pl.ds(i * per, per)] = got.astype(BF).reshape(per, G * 8, W)

            def send(q):
                zz = i * per + q

                @pl.when(zz != z)
                def _():
                    remote(pooled.at[zz], mid_p.at[z // M], 3, dp_of(g, zz), m)

                @pl.when(zz == z)
                def _():
                    local(pooled.at[zz], mid_p.at[z // M], 3)

            each(0, per, send)

        each(0, NS // CH, pool)

    sent_if(conc, lambda: wait_out(pooled.at[pl.ds(0, Z - 1)], 3))
    ins["pooled"] = lambda: wait_in(mid_p, 3)

    take("pooled")
    send_p[...] = dot(swap_ref[0], mid_p[...].reshape(R2, W)).astype(BF).reshape(G, K * 8, W)
    local(send_p.at[g], slots.at[m * G + g], 4)

    for dp, gg, mm in near:
        remote(send_p.at[gg], slots.at[m * G + g], 4, dp, mm)
    sent(slots.at[pl.ds(0, M * G - 1)], 4)
    ins["slots"] = lambda: wait_in(slots, 4)
    take("slots")

    for i in (5, 6, 9, 10, 11):
        loads[i].wait()
    table_s = slots[...].reshape(NS, W)
    feat[0] = dense_ref[...]
    for f in range(3):
        feat[f + 1] = dot(from_slot[f], table_s).astype(BF)
    features = jnp.concatenate([feat[i] for i in range(4)], axis=1)
    pre = dot(features, w_ref[...]) + b_ref[...]
    sig = jax.nn.sigmoid(pre)
    active = pre * sig
    act[...] = active
    slope[...] = sig * (1.0 + pre * (1.0 - sig)) * wo_ref[...]
    part = jnp.sum(active * wo_ref[...], axis=1, keepdims=True)
    eye_b = iota((B, B), 0) == iota((B, B), 1)
    part_row = jnp.sum(jnp.where(eye_b, part, 0.0), axis=0, keepdims=True)
    lbuf[m] = jnp.broadcast_to(part_row, (8, B))
    each(1, M, lambda t: remote(lbuf.at[m], lbuf.at[m], 3, me, lax.rem(m + t, M), True))
    sent(lbuf.at[pl.ds(0, M - 1)], 3, True)
    ins["logits"] = lambda: wait_in(lbuf.at[pl.ds(0, M - 1)], 3, True)
    eye_w = onehot(iota((W, W), 0) == iota((W, W), 1))
    for i in range(4):
        turned = dot(eye_w, feat[i], ((1,), (1,))).astype(BF)
        feat_t[i // 2, pl.ds((i % 2) * W, W), :] = turned
    take("logits")

    total = lbuf[0]
    for i in range(1, M):
        total = total + lbuf[i]
    lgrad_row = jax.nn.sigmoid(total[0:1, :]) - label_ref[...].astype(F32)
    lgrad = to_col(lgrad_row, B, eye_b)
    grad_pre = lgrad * slope[...]
    grad_low = grad_pre.astype(BF)
    hrows = 512 // C
    other = 1 - c
    mate = me + 1 - 2 * c

    for q in range(S.Q):
        send_c[q] = dot(feat_t[other], grad_low[:, q * S.HQ : (q + 1) * S.HQ]).astype(BF)
        remote(send_c.at[q], recv_c.at[q], 16 + q, mate, m)
        sent(send_c.at[q], 16 + q)
        ins["core", q] = lambda q=q: wait_in(recv_c.at[q], 16 + q)
    for q in range(S.Q):
        keep_c[q] = dot(feat_t[c], grad_low[:, q * S.HQ : (q + 1) * S.HQ])

    for f in range(3):
        term = dot(grad_low, w_ref[pl.ds((f + 1) * W, W), :], ((1,), (1,)))
        inputs[pl.ds(f * B, B), :] = term.astype(BF)
    for q in range(S.Q):
        take(("core", q))
        keep_y[q] = keep_c[q] + recv_c[q].astype(F32)
        send_y[q] = keep_y[q].astype(BF).reshape(Y, S.RY, S.HQ)

        def to_y(t):
            yy = lax.rem(y + t, Y)
            remote(send_y.at[q, yy], recv_y.at[q, y], 18 + q, (yy * Z + z) * C + c, m)

        each(1, Y, to_y)
        sent(send_y.at[q, pl.ds(0, Y - 1)], 18 + q)
        ins["dense_y", q] = lambda q=q: wait_in(recv_y.at[q, pl.ds(0, Y - 1)], 18 + q)
    for q in range(M):
        part_s[q] = dot(to_slot[q], inputs[...]).astype(BF).reshape(G, K * 8, W)

    local(part_s.at[m, g], recv_x.at[m * G + g], 7)
    for dp, gg, mm in near:
        remote(part_s.at[mm, gg], recv_x.at[m * G + g], 7, dp, mm)
    sent(recv_x.at[pl.ds(0, M * G - 1)], 7)
    ins["bags_x"] = lambda: wait_in(recv_x, 7)

    b1 = jnp.sum(grad_pre, axis=0, keepdims=True)
    w2 = jnp.sum(lgrad * act[...], axis=0, keepdims=True)
    for i, row in enumerate((b1, w2)):
        for j in range(HL // W):
            vec[i, j // S.V, pl.ds(j % S.V, 1), :] = row[:, j * W : (j + 1) * W]

    remote(vec.at[other], vec_c.at[pl.ds(0, Y)], 6, mate, m, True)
    sent(vec_c.at[pl.ds(0, Y)], 6, True)
    ins["core_v"] = lambda: wait_in(vec_c.at[pl.ds(0, Y)], 6, True)


    take("core_v")
    vec[c] = vec[c] + vec_c[pl.ds(0, Y)]

    def to_y_vec(t):
        yy = lax.rem(y + t, Y)
        remote(vec.at[c, yy], vec_y.at[y], 8, (yy * Z + z) * C + c, m, True)

    each(1, Y, to_y_vec)
    sent(vec_y.at[pl.ds(0, Y - 1)], 8, True)
    ins["dense_yv"] = lambda: wait_in(vec_y.at[pl.ds(0, Y - 1)], 8, True)

    def dense_z(q):
        take(("dense_y", q))
        acc = keep_y[q, pl.ds(pl.multiple_of(y * S.RY, S.RY), S.RY), :]
        for t in range(1, Y):
            acc = acc + recv_y[q, lax.rem(y + t, Y)].astype(F32)
        for i in range(Z):
            r0, c0 = (i // S.CG) * S.pr, (i % S.CG) * S.pc
            send_z[q, i] = acc[r0 : r0 + S.pr, c0 : c0 + S.pc].astype(BF)
        local(send_z.at[q, z], recv_z.at[q, z], 20 + q)

        def to_z(zz):
            remote(send_z.at[q, zz], recv_z.at[q, z], 20 + q, dp_of(g, zz), m)

        along_z(to_z)
        sent(send_z.at[q, pl.ds(0, Z - 1)], 20 + q)
        ins["dense_z", q] = lambda: wait_in(recv_z.at[q], 20 + q)

    for q in range(S.Q):
        dense_z(q)

    take("bags_x")
    total = recv_x[pl.ds(0, G)].astype(F32)
    for i in range(1, M):
        total = total + recv_x[pl.ds(i * G, G)].astype(F32)
    send_h[...] = dot(swap_ref[1], total.astype(BF).reshape(R2, W)).astype(BF).reshape(K, G * 8, W)

    def grad_b(k):
        zz = base_z + M * k

        @pl.when(zz != z)
        def _():
            remote(send_h.at[k], recv_g.at[z], 11, dp_of(g, zz), m)

        @pl.when(zz == z)
        def _():
            local(send_h.at[k], recv_g.at[z], 11)

    each(0, K, grad_b)

    def grad_b_sent(n):
        if n:
            wait_out(send_h.at[pl.ds(0, n)], 11)

    sent_if(conc, lambda: grad_b_sent(K - 1))
    sent_if(jnp.logical_not(conc), lambda: grad_b_sent(K))
    ins["grads"] = lambda: pl.when(conc)(lambda: wait_in(recv_g, 11))


    take("dense_yv")
    accv = vec[c, y]
    for t in range(1, Y):
        accv = accv + vec_y[lax.rem(y + t, Y)]
    vec_ys[0] = accv
    local(vec_ys.at[0], vec_z.at[z], 10, True)
    along_z(lambda zz: remote(vec_ys.at[0], vec_z.at[z], 10, dp_of(g, zz), m, True))
    sent(vec_z.at[pl.ds(0, Z - 1)], 10, True)
    ins["dense_zv"] = lambda: wait_in(vec_z.at[pl.ds(0, Z)], 10, True)
    def cast_t():
        for h in range(2):
            part = recv_t.at[pl.ds(h * (Z // 2), Z // 2)]
            each(1, M, lambda t: remote(part, part, 2, me, lax.rem(m + t, M)))

    def cast_t_sent():
        for _ in range(M - 1):
            wait_out(recv_t, 2)

    pl.when(conc)(cast_t)
    sent_if(conc, cast_t_sent)
    ins["cast_t"] = lambda: pl.when(jnp.logical_not(conc))(lambda: wait_in(recv_t, 2))


    block0 = c * hrows + y * S.RY

    def gather_z(q):
        take(("dense_z", q))

        sums = [recv_z[q, i].astype(F32) for i in range(Z)]
        while len(sums) > 1:
            sums = [a + b for a, b in zip(sums[0::2], sums[1::2])]
        acc = sums[0]
        r0 = pl.multiple_of(block0 + (z // S.CG) * S.pr, 16)
        c0 = pl.multiple_of(q * S.HQ + lax.rem(z, S.CG) * S.pc, W)
        out_w[pl.ds(r0, S.pr), pl.ds(c0, S.pc)] = acc.astype(BF)
        piece = out_w.at[pl.ds(r0, S.pr), pl.ds(c0, S.pc)]
        along_z(lambda zz: remote(piece, piece, 22 + q, dp_of(g, zz), m))
        sent(send_z.at[q, pl.ds(0, Z - 1)], 22 + q)
        ins["out_z", q] = lambda: wait_in(send_z.at[q, pl.ds(0, Z - 1)], 22 + q)


    for q in range(S.Q):
        gather_z(q)
    take("cast_r")
    sel = onehot((iota((16, W), 1) & 15) == iota((16, W), 0))
    lists = dot(sel, entries(0, NS), ((1,), (1,)))
    list8 = lists[0:8, :]
    slot_row = lists[8:9, :]
    take("grads")

    @pl.when(conc)
    def _():
        each(1, M, lambda t: remote(recv_g, recv_g, 13, me, lax.rem(m + t, M)))

    def grads_sent():
        for _ in range(M - 1):
            wait_out(recv_g, 13)

    sent_if(conc, grads_sent)
    ins["grads_x"] = lambda: pl.when(jnp.logical_not(conc))(lambda: wait_in(recv_g, 13))

    take("dense_zv")
    accv = vec_z[0]
    for i in range(1, Z):
        accv = accv + vec_z[i]
    out_v[c, y] = accv

    def ag_yv(t):
        yy = lax.rem(y + t, Y)
        remote(out_v.at[c, y], out_v.at[c, y], 14, (yy * Z + z) * C + c, m, True)

    each(1, Y, ag_yv)
    sent(out_v.at[0, pl.ds(0, Y - 1)], 14, True)
    ins["out_yv"] = lambda: wait_in(out_v.at[0, pl.ds(0, Y - 1)], 14, True)

    QR = G * 16

    def update(pair):
        for i in (2 * pair, 2 * pair + 1):
            update_one(i)

    def update_one(i):
        row = iota((QR, 1), 0)
        slot_id = (lax.shift_right_logical(row, 3) + i * (QR // 8)).astype(F32)
        cnt = jnp.broadcast_to(list8[None], (QR // 8, 8, NS)).reshape(QR, NS)
        wide = jnp.where(slot_row == slot_id, cnt, 0.0).astype(BF)
        grad = dot(wide, recv_g[...].reshape(NS, W))
        src_rows = recv_r[i]
        wide_s = jnp.broadcast_to(src_rows[:, None, :], (G, 16, W)).reshape(QR, W)
        pick_s = iota((QR, W), 1) == (iota((QR, W), 0) & 15) + 96
        st = jnp.sum(jnp.where(pick_s, wide_s, 0.0), axis=1, keepdims=True)
        st = st + jnp.sum(grad * grad, axis=1, keepdims=True) * (1.0 / W)
        low = recv_t[i].reshape(QR, W).astype(F32)
        new = low - learn_rate * grad / (jnp.sqrt(st) + epsilon)
        pick_o = iota((QR, W), 1) == (iota((QR, W), 0) & 7)
        st8 = jnp.sum(jnp.where(pick_o, st, 0.0).reshape(QR // 8, 8, W), axis=1)
        for q in range(Y):
            at = pl.ds(pl.multiple_of((q * Z + i) * 32, 32), 32)
            out_t[at, :] = new[q * 32 : (q + 1) * 32]
            stage_s[pl.ds((q * Z + i) * 4, 4), :] = st8[q * 4 : (q + 1) * 4]

    for q in range(S.Q):
        take(("out_z", q))
        mine = out_w.at[pl.ds(pl.multiple_of(block0, 16), S.RY), pl.ds(q * S.HQ, S.HQ)]

        def ag_y(t):
            yy = lax.rem(y + t, Y)
            remote(mine, mine, 24 + q, (yy * Z + z) * C + c, m)

        each(1, Y, ag_y)
        sent(send_y.at[q, pl.ds(0, Y - 1)], 24 + q)
        ins["out_y", q] = lambda q=q: wait_in(send_y.at[q, pl.ds(0, Y - 1)], 24 + q)

    take("cast_t")
    take("grads_x")
    each(0, Z // 2, update)

    writes = []

    def write(src, dst, i):
        writes.append(pltpu.make_async_copy(src, dst, out_sem.at[i]))
        writes[-1].start()

    write(out_t, results[0], 0)

    def gather_core(q):
        take(("out_y", q))
        part = out_w.at[pl.ds(pl.multiple_of(c * hrows, 16), hrows), pl.ds(q * S.HQ, S.HQ)]
        remote(part, part, 26 + q, mate, m)
        sent(send_c.at[q], 26 + q)
        ins["out_c", q] = lambda: wait_in(recv_c.at[q], 26 + q)

    for q in range(S.Q):
        gather_core(q)
    take("out_yv")
    remote(out_v.at[c], out_v.at[c], 15, mate, m, True)
    sent(vec_c.at[pl.ds(0, Y)], 15, True)
    ins["out_cv"] = lambda: wait_in(vec_c.at[pl.ds(0, Y)], 15, True)
    own = pl.ds(pl.multiple_of(c * hrows, 16), hrows)
    write(out_w.at[own], results[2].at[own], 3)
    out_s[...] = jnp.transpose(stage_s[pl.ds(0, NB), :])[0:8, :]
    write(out_s, results[1], 2)
    take("out_cv")
    for q in range(S.Q):
        take(("out_c", q))
    far = pl.ds(pl.multiple_of(other * hrows, 16), hrows)
    write(out_w.at[far], results[2].at[far], 4)
    write(out_v.at[pl.ds(0, C)], results[3], 5)
    assert not ins
    for copy in writes:
        copy.wait()

    for done in outs:
        done()


def local_step(
    dense_input,
    labels,
    table,
    adagrad_state,
    new_owner,
    bag_owner,
    bag_slot,
    bag_offsets,
    bag_length,
    w_first,
    b_first,
    w_out,
):
    blocks = table.shape[0]
    samples = dense_input.shape[0]
    hidden = w_first.shape[1]
    S = Shape(lax.axis_size("dp"), lax.axis_size("mp"), blocks, samples, hidden)
    C, Y, Z, M, K, G, N = S.C, S.Y, S.Z, S.M, S.K, S.G, S.N
    R2 = K * G * 8
    V = pltpu.VMEM
    hrows = 512 // C
    args = (
        new_owner.reshape(1, blocks),
        bag_owner.reshape(1, 3 * samples),
        bag_slot,
        bag_offsets.T,
        bag_length,
        dense_input,
        labels.reshape(1, samples),
        table.reshape(blocks * 8, W),
        adagrad_state.T,
        w_first,
        b_first.reshape(1, hidden),
        w_out.reshape(1, hidden),
    )
    made = (
        jax.ShapeDtypeStruct((blocks * 8, W), F32),
        jax.ShapeDtypeStruct((8, blocks), F32),
        jax.ShapeDtypeStruct((512, hidden), BF),
        jax.ShapeDtypeStruct((C, Y, S.V, W), F32),
    )
    found = pl.pallas_call(
        functools.partial(kernel, S),
        out_shape=made,
        in_specs=[pl.BlockSpec(memory_space=pltpu.HBM)] * 12,
        out_specs=(pl.BlockSpec(memory_space=pl.ANY),) * 4,
        scratch_shapes=[
            V((blocks + 8, W), F32),
            V((2 * S.T * 8 + 8, W), F32),
            V((G, K, 16, W), BF),
            V((G + 8, K, 1, W), F32),
            V((G, K, 16, W), BF),
            V((G + 8, K, 1, W), F32),
            V((K + 1, G, W), F32),
            V((Z, G, 16, W), BF),
            V((Z, G, W), F32),
            V((Z, G * 8, W), BF),
            V((K, G * 8, W), BF),
            V((G, K * 8, W), BF),
            V((M * G, K * 8, W), BF),
            V((M, 8, samples), F32),
            V((samples, hidden), F32),
            V((samples, hidden), F32),
            V((4, samples, W), BF),
            V((C, 2 * W, samples), BF),
            V((3, samples, S.N * 8), BF),
            V((M, R2, 3 * samples), BF),
            V((2, R2, R2), BF),
            V((3 * samples, W), BF),
            V((M, G, K * 8, W), BF),
            V((M * G, K * 8, W), BF),
            V((K, G * 8, W), BF),
            V((Z, G * 8, W), BF),
            V((S.Q, hrows, S.HQ), BF),
            V((S.Q, hrows, S.HQ), F32),
            V((S.Q, hrows, S.HQ), BF),
            V((S.Q, Y, S.RY, S.HQ), BF),
            V((S.Q, hrows, S.HQ), F32),
            V((S.Q, Y, S.RY, S.HQ), BF),
            V((S.Q, Z, S.pr, S.pc), BF),
            V((S.Q, Z, S.pr, S.pc), BF),
            V((C + 2, Y, S.V, W), F32),
            V((Y + 8, S.V, W), F32),
            V((Y + 8, S.V, W), F32),
            V((8, S.V, W), F32),
            V((Z + 8, S.V, W), F32),
            pltpu.SemaphoreType.DMA((32,)),
            pltpu.SemaphoreType.DMA((32,)),
            pltpu.SemaphoreType.DMA((32,)),
            pltpu.SemaphoreType.DMA((32,)),
            pltpu.SemaphoreType.DMA((12,)),
            pltpu.SemaphoreType.DMA((6,)),
        ]
        + [V((a.shape[0] + 8, W) if a.shape == (blocks * 8, W) else a.shape, a.dtype) for a in args]
        + [V(a.shape, a.dtype) for a in made[:3]]
        + [V((C + 2, Y, S.V, W), F32)],
        compiler_params=pltpu.CompilerParams(
            collective_id=0, has_side_effects=True, vmem_limit_bytes=56 * 1024 * 1024
        ),
    )(*args)
    part = jax.ShapeDtypeStruct((Y, S.V, W), F32)
    out_t, out_s, out_w, b1, w2 = pl.pallas_call(
        hand_over,
        out_shape=(*made[:3], part, part),
        in_specs=[pl.BlockSpec(memory_space=pl.ANY)] * 4,
        out_specs=(pl.BlockSpec(memory_space=pl.ANY),) * 5,
        scratch_shapes=[V(a.shape, a.dtype) for a in made]
        + [pltpu.SemaphoreType.DMA((11,)), pltpu.SemaphoreType.DMA((11,))],
    )(*found)
    return (
        out_t.reshape(blocks, 8, W),
        out_s.T,
        out_w,
        b1.reshape(hidden),
        w2.reshape(hidden),
    )


def hand_over(t, s, w, v, out_t, out_s, out_w, out_b, out_u, vm_t, vm_s, vm_w, vm_v, sem_in, sem_out):
    trips = []
    for a, x, b in ((t, vm_t, out_t), (w, vm_w, out_w)):
        n = a.shape[0] // 4
        cuts = [pl.ds(i * n, n) for i in range(4)]
        trips += [(a.at[p], x.at[p], b.at[p]) for p in cuts]
    trips += [(s, vm_s, out_s), (v.at[0], vm_v.at[0], out_b), (v.at[1], vm_v.at[1], out_u)]
    come = [pltpu.make_async_copy(a, x, sem_in.at[i]) for i, (a, x, _) in enumerate(trips)]
    go = [pltpu.make_async_copy(x, b, sem_out.at[i]) for i, (_, x, b) in enumerate(trips)]
    for copy in come:
        copy.start()
    for first, then in zip(come, go):
        first.wait()
        then.start()
    for copy in go:
        copy.wait()


def solution(mesh):
    placed = (
        P("dp", None),
        P("dp"),
        P("dp", None, None),
        P("dp", None),
        P("dp"),
        P("dp", None),
        P("dp"),
        P("dp", None),
        P("dp"),
        P(None, "mp"),
        P("mp"),
        P("mp"),
    )
    return jax.shard_map(
        local_step,
        mesh=mesh,
        in_specs=placed,
        out_specs=(P("dp", None, None), P("dp", None), P(None, "mp"), P("mp"), P("mp")),
        check_vma=False,
    )
```
